32 devices in a mesh: seq: 8 (over z, x), diag: 4 (over y, core).
Axes of the slice: x: 2, y: 2, z: 4, core: 2. Of those that a mesh axis runs over, the one named last changes fastest.
Arguments:
- seq_feat: bfloat16 [512, 128], P('seq'), may hold values from -6 to 6
- conv1_weight: bfloat16 [2, 3, 128, 128], replicated, may hold values from -0.3125 to 0.3125
- conv2_kernel_weight: bfloat16 [3, 3, 128, 128], replicated, may hold values from -0.1875 to 0.1875
- dilations: int32 [3], replicated, may hold values from 1 to 8, as said below
- block_mask: int32 [8, 8], P('seq', 'diag'), may hold values 0 or 1
- band_grad: bfloat16 [512, 512, 128], P('seq', 'diag'), may hold values from -0.5 to 0.5
Outputs:
- band_out: bfloat16 [512, 512, 128], P('seq', 'diag')
- seq_grad: float32 [512, 128], P('seq')
- conv1_grad: float32 [2, 3, 128, 128], replicated
- conv2_grad: float32 [3, 3, 128, 128], replicated
The draws below stay inside these ranges and needn't reach their ends.
Inputs may be any that keep to these rules, and one draw needn't show every extreme that they name: `dilations`: one entry equals 8.
All inputs are finite; a program needn't handle non-finite values. No bound on the sum of `block_mask` on one device may be relied on, other than what follows from the above.
Results may differ from the reference program's by a relative error of at most 0.014.
Values may be sent and summed in bfloat16 or wider, within the bound.
A program may use at most 128 MiB of HBM per device.

```python
import math
import jax
import jax.numpy as jnp
from jax import lax

CHANNELS = 128
BAND = 512
BLOCK = 64
MAXDIL = 8
LINE_LAYERS = 2
SEQ_BINS = 512
BLOCKS = 8
BAND_BLOCKS = 8


def draw_dilations(key, part):
    first_key, second_key = jax.random.split(key)
    values = jax.random.randint(first_key, (LINE_LAYERS + 1,), 1, MAXDIL + 1)
    chosen = jax.random.randint(second_key, (), 0, LINE_LAYERS + 1)
    places = jnp.arange(LINE_LAYERS + 1)
    return jnp.where(places == chosen, MAXDIL, values).astype(jnp.int32)


def with_ends(result, key, smallest, largest):
    spot = [jax.random.randint(jax.random.fold_in(key, axis), (), 0, length) for axis, length in enumerate(result.shape)]
    widest = result.shape.index(max(result.shape))
    next_to = spot[:widest] + [(spot[widest] + 1) % result.shape[widest]] + spot[widest + 1:]
    return result.at[tuple(spot)].set(smallest).at[tuple(next_to)].set(largest)


def block_scale(stream_key, shape, shards, least, largest):
    factor_of, own = 1.0, jax.random.fold_in(stream_key, 6)
    for axis_at, blocks in shards:
        draws = jnp.exp(jax.random.uniform(jax.random.fold_in(own, axis_at), (blocks,), jnp.float32, least / len(shards), largest / len(shards)))
        factor_of = factor_of * jnp.repeat(draws, shape[axis_at] // blocks).reshape([-1 if axis == axis_at else 1 for axis in range(len(shape))])
    return factor_of


def noise(own_key, extent, deviation, reach, pieces=(), kind=jnp.bfloat16):
    loudness = block_scale(own_key, extent, pieces, -0.22, 0.18) if pieces else 1.0
    entries = jax.random.normal(own_key, extent, jnp.float32) * deviation * loudness
    return jnp.minimum(jnp.maximum(entries, -reach), reach).astype(kind)


def setup_inputs(seed: int = 0) -> dict:
    key_list = jax.random.split(jax.random.key(seed), 7)
    return {
        "seq_feat": noise(key_list[0], (SEQ_BINS, CHANNELS), 1.0, 6.0, ((0, 8),)),
        "conv1_weight": noise(key_list[1], (LINE_LAYERS, 3, CHANNELS, CHANNELS), (3 * CHANNELS) ** -0.5, 0.3125),
        "conv2_kernel_weight": noise(key_list[2], (3, 3, CHANNELS, CHANNELS), (9 * CHANNELS) ** -0.5, 0.1875),
        "dilations": draw_dilations(jax.random.fold_in(key_list[6], 71), 0),
        "block_mask": with_ends((jax.random.randint(key_list[4], (BLOCKS, BAND_BLOCKS), 0, 4) < 3).astype(jnp.int32), jax.random.fold_in(key_list[4], 1), 0, 1),
        "band_grad": noise(key_list[5], (SEQ_BINS, BAND, CHANNELS), ((2 * BAND) ** -0.5), 0.5, ((0, 8), (1, 4))),
    }


root_half = 0.7071067811865476
inv_root_two_pi = 0.3989422804014327

def gelu_value(values):
    return 0.5 * values * (1.0 + lax.erf(values * root_half))

def gelu_slope(values):
    return 0.5 * (1.0 + lax.erf(values * root_half)) + values * jnp.exp(-0.5 * values * values) * inv_root_two_pi

def line_taps(margin_extended, weights, spacing_factor, direction, length):
    running = jnp.zeros((length, weights.shape[-1]), jnp.float32)
    for tap_index in range(3):
        row_start = MAXDIL + direction * (tap_index - 1) * spacing_factor
        slab_piece = lax.dynamic_slice_in_dim(margin_extended, row_start, length, 0)
        running = running + jnp.dot(slab_piece, weights[tap_index], preferred_element_type=jnp.float32)
    return running

def line_terms(margin_extended, upstream_sensitivity, spacing_factor, length):
    tap_terms = []
    for tap_index in range(3):
        slab_piece = lax.dynamic_slice_in_dim(margin_extended, MAXDIL + (tap_index - 1) * spacing_factor, length, 0)
        tap_terms.append(lax.dot_general(slab_piece, upstream_sensitivity, (((0,), (0,)), ((), ())), preferred_element_type=jnp.float32))
    return jnp.stack(tap_terms)

def plane_kernel_taps(margin_extended, weights, spacing_factor, direction):
    block_rows = math.gcd(SEQ_BINS, 512)

    def one_block(first_row):
        region = lax.dynamic_slice_in_dim(margin_extended, first_row, block_rows + 2 * MAXDIL, 0)
        running = jnp.zeros((block_rows * BAND, CHANNELS), jnp.float32)
        for row_tap in range(3):
            for col_tap in range(3):
                row_start = MAXDIL + direction * (row_tap - 1) * spacing_factor
                col_start = MAXDIL + direction * (col_tap - 1) * spacing_factor
                slab_piece = lax.dynamic_slice(region, (row_start, col_start, jnp.int32(0)), (block_rows, BAND, CHANNELS))
                running = running + jnp.dot(slab_piece.reshape(block_rows * BAND, CHANNELS), weights[row_tap, col_tap], preferred_element_type=jnp.float32)
        return running.reshape(block_rows, BAND, CHANNELS)
    starts = (jnp.arange(SEQ_BINS // block_rows) * block_rows).astype(jnp.int32)
    return lax.map(one_block, starts).reshape(SEQ_BINS, BAND, CHANNELS)

def surface_contribution_list(margin_extended, upstream_sensitivity, spacing_factor):
    block_rows = math.gcd(SEQ_BINS, 512)

    def one_block(first_row):
        region = lax.dynamic_slice_in_dim(margin_extended, first_row, block_rows + 2 * MAXDIL, 0)
        grad_block = lax.dynamic_slice_in_dim(upstream_sensitivity, first_row, block_rows, 0).reshape(block_rows * BAND, CHANNELS)
        tap_terms = []
        for row_tap in range(3):
            for col_tap in range(3):
                row_start = MAXDIL + (row_tap - 1) * spacing_factor
                col_start = MAXDIL + (col_tap - 1) * spacing_factor
                slab_piece = lax.dynamic_slice(region, (row_start, col_start, jnp.int32(0)), (block_rows, BAND, CHANNELS))
                tap_terms.append(lax.dot_general(slab_piece.reshape(block_rows * BAND, CHANNELS), grad_block, (((0,), (0,)), ((), ())), preferred_element_type=jnp.float32))
        return jnp.stack(tap_terms).reshape(3, 3, CHANNELS, CHANNELS)
    starts = (jnp.arange(SEQ_BINS // block_rows) * block_rows).astype(jnp.int32)
    return lax.optimization_barrier(jnp.sum(lax.map(one_block, starts), axis=0))

def reference(seq_feat, conv1_weight, conv2_kernel_weight, dilations, block_mask, band_grad):
    hidden = seq_feat
    stored_layers = []
    for layer_index in range(LINE_LAYERS):
        active = gelu_value(hidden.astype(jnp.float32)).astype(jnp.bfloat16)
        margin_extended = jnp.pad(active, ((MAXDIL, MAXDIL), (0, 0)))
        filtered_output = line_taps(margin_extended, conv1_weight[layer_index], dilations[layer_index], 1, SEQ_BINS)
        stored_layers.append((hidden, margin_extended))
        hidden = (hidden.astype(jnp.float32) + filtered_output).astype(jnp.bfloat16)
    extended = jnp.concatenate([hidden, jnp.zeros((BAND, CHANNELS), jnp.bfloat16)], axis=0)
    partner = jax.vmap(lambda row_index: lax.dynamic_slice_in_dim(extended, row_index, BAND, 0))(jnp.arange(SEQ_BINS).astype(jnp.int32))
    cell_mask = jnp.repeat(jnp.repeat(block_mask, BLOCK, axis=0), BLOCK, axis=1).astype(jnp.float32)[:, :, None]
    band_in = (cell_mask * 0.5 * (hidden.astype(jnp.float32)[:, None, :] + partner.astype(jnp.float32))).astype(jnp.bfloat16)
    plane_act = gelu_value(band_in.astype(jnp.float32)).astype(jnp.bfloat16)
    border = ((MAXDIL, MAXDIL), (MAXDIL, MAXDIL), (0, 0))
    framed_response = jnp.pad(plane_act, border)
    surface_spacing = dilations[LINE_LAYERS]
    filtered_output = plane_kernel_taps(framed_response, conv2_kernel_weight, surface_spacing, 1)
    band_out = (cell_mask * (band_in.astype(jnp.float32) + filtered_output)).astype(jnp.bfloat16)
    slope_masked_derivative = (cell_mask * band_grad.astype(jnp.float32)).astype(jnp.bfloat16)
    surface_accumulated = surface_contribution_list(framed_response, slope_masked_derivative, surface_spacing)
    bordered_gradient = jnp.pad(slope_masked_derivative, border)
    reverse_activation = plane_kernel_taps(bordered_gradient, jnp.swapaxes(conv2_kernel_weight, 2, 3), surface_spacing, -1)
    band_in_grad = slope_masked_derivative.astype(jnp.float32) + gelu_slope(band_in.astype(jnp.float32)) * reverse_activation
    tile_grad = (0.5 * cell_mask * band_in_grad).astype(jnp.bfloat16)
    row_part = lax.optimization_barrier(jnp.sum(tile_grad, axis=1, dtype=jnp.float32))

    def add_column(offset, running):
        column = lax.dynamic_index_in_dim(tile_grad, offset, 1, keepdims=False).astype(jnp.float32)
        extended_col = jnp.concatenate([jnp.zeros((BAND, CHANNELS), jnp.float32), column], axis=0)
        return running + lax.dynamic_slice_in_dim(extended_col, BAND - offset, SEQ_BINS, 0)
    column_part = lax.fori_loop(jnp.int32(0), jnp.int32(BAND), add_column, jnp.zeros((SEQ_BINS, CHANNELS), jnp.float32))
    gradient = row_part + column_part
    tower_list = [None] * LINE_LAYERS
    for layer_index in reversed(range(LINE_LAYERS)):
        layer_hidden, margin_extended = stored_layers[layer_index]
        spacing_factor = dilations[layer_index]
        grad_bf = gradient.astype(jnp.bfloat16)
        tower_list[layer_index] = line_terms(margin_extended, grad_bf, spacing_factor, SEQ_BINS)
        padded_line = jnp.pad(grad_bf, ((MAXDIL, MAXDIL), (0, 0)))
        backward_line = line_taps(padded_line, jnp.swapaxes(conv1_weight[layer_index], 1, 2), spacing_factor, -1, SEQ_BINS)
        gradient = gradient + gelu_slope(layer_hidden.astype(jnp.float32)) * backward_line
    scaling = 1.0 / math.sqrt(SEQ_BINS)
    return (band_out, gradient, jnp.stack(tower_list) * scaling, surface_accumulated * scaling)
```

```python
import functools
import math

import jax
import jax.numpy as jnp
from jax import lax
from jax.experimental import pallas as pl
from jax.experimental.pallas import tpu as pltpu
from jax.sharding import PartitionSpec as P

BLOCK = 64
HALO = 8
LINE_LAYERS = 2
HOFF = 16
MESH = pl.DeviceIdType.MESH

root_half = 0.7071067811865476
inv_root_two_pi = 0.3989422804014327

F32 = jnp.float32
BF16 = jnp.bfloat16


def rounded(x):
    return x.astype(BF16).astype(F32)


def gelu_pair(v):
    half = 0.5 * (1.0 + lax.erf(v * root_half))
    return v * half, half


def slope_from(v, half):
    return half + v * jnp.exp(-0.5 * v * v) * inv_root_two_pi


def dot(a, b, dims=((1,), (0,))):
    return lax.dot_general(a, b, (dims, ((), ())), preferred_element_type=F32)


def owners_for(units, devices):
    return max(n for n in range(1, devices + 1) if units % n == 0)


def kernel(
    S, D, R, B, C, NOWN,
    feat_ref, w1_ref, w2_ref, dil_ref, mask_ref, grad_ref,
    out_ref, seqg_ref, c1_ref, c2_ref,
    feat_all, hid, h1, acts, maskt, mrow, wide, p3, g3, slope, bandin, w2t,
    top, bottom, left, right, corner,
    wg, wsend, wrecv, wsum, wall, rowpart, colpart, gslots, gmine, gall, gpad,
    s_feat, r_feat, s_halo, r_halo, s_mask, r_mask, s_ws, r_ws, s_wa, r_wa,
    s_g, r_g, s_ga, r_ga,
):
    N = R * S
    W = B * D
    NDEV = S * D
    PIECE = 9 * C // NOWN
    RATIO = B // R
    Q = R // D
    s = lax.axis_index("seq")
    d = lax.axis_index("diag")
    me = s * D + d
    row0 = s * R
    d0 = d * B
    e2 = dil_ref[LINE_LAYERS]

    def device(index):
        return (index // D, index % D)

    def copy(src, dst, ss, rs, dev):
        return pltpu.make_async_remote_copy(
            src_ref=src, dst_ref=dst, send_sem=ss, recv_sem=rs,
            device_id=dev, device_id_type=MESH,
        )

    for k in range(2):
        value = mask_ref[0, k].astype(F32)
        maskt[1, 1, 8 * k : 8 * k + 8, :] = jnp.full((8, C), 1.0, F32) * value

    barrier = pltpu.get_barrier_semaphore()

    @pl.loop(1, NDEV)
    def _(step):
        pl.semaphore_signal(
            barrier, inc=1, device_id=device(lax.rem(me + step, NDEV)), device_id_type=MESH
        )

    pl.semaphore_wait(barrier, NDEV - 1)

    def feat_copy(other):
        return copy(
            feat_ref, feat_all.at[pl.ds(pl.multiple_of(row0, R), R)],
            s_feat.at[other], r_feat.at[s], (other, d),
        )

    @pl.loop(1, S)
    def _(step):
        feat_copy(lax.rem(s + step, S)).start()

    neighbours = [(a, b) for a in (-1, 0, 1) for b in (-1, 0, 1) if (a, b) != (0, 0)]

    def exists(a, b):
        return (s + a >= 0) & (s + a < S) & (d + b >= 0) & (d + b < D)

    def mask_copy(a, b):
        return copy(
            maskt.at[1, 1], maskt.at[1 - a, 1 - b],
            s_mask.at[1 + a, 1 + b], r_mask.at[1 - a, 1 - b], (s + a, d + b),
        )

    def halo_slot(a, b):
        if b == 0:
            return top if a < 0 else bottom
        if a == 0:
            return left if b < 0 else right
        return corner.at[(1 + a) // 2, (1 + b) // 2]

    def halo_copy(a, b):
        rows = {-1: pl.ds(0, HALO), 0: pl.ds(0, R), 1: pl.ds(R - HALO, HALO)}[a]
        cols = {-1: pl.ds(0, 16), 0: pl.ds(0, B), 1: pl.ds(B - 16, 16)}[b]
        return copy(
            grad_ref.at[rows, cols], halo_slot(-a, -b),
            s_halo.at[1 + a, 1 + b], r_halo.at[1 - a, 1 - b], (s + a, d + b),
        )

    for a, b in neighbours:
        @pl.when(exists(a, b))
        def _():
            mask_copy(a, b).start()

    for a, b in neighbours:
        @pl.when(exists(a, b))
        def _():
            halo_copy(a, b).start()

        @pl.when(jnp.logical_not(exists(a, b)))
        def _():
            maskt[1 + a, 1 + b] = jnp.zeros((16, C), F32)
            slot = halo_slot(a, b)
            slot[...] = jnp.zeros(slot.shape, BF16)

    feat_all[pl.ds(pl.multiple_of(row0, R), R), :] = feat_ref[...]
    hid[0:HOFF, :] = jnp.zeros((HOFF, C), F32)
    hid[HOFF + N :, :] = jnp.zeros((hid.shape[0] - HOFF - N, C), F32)
    for layer in range(LINE_LAYERS):
        acts[layer, 0:HALO, :] = jnp.zeros((HALO, C), F32)
        acts[layer, HALO + N :, :] = jnp.zeros((HALO, C), F32)
    gpad[0:HALO, :] = jnp.zeros((HALO, C), F32)
    gpad[HALO + N :, :] = jnp.zeros((HALO, C), F32)
    for a in range(3):
        for b in range(3):
            w2t[a, b * C : (b + 1) * C, :] = w2_ref[a, b].astype(F32).T.astype(BF16)
    wg[...] = jnp.zeros(wg.shape, F32)
    colpart[...] = jnp.zeros(colpart.shape, F32)

    @pl.loop(1, S)
    def _(step):
        other = lax.rem(s + step, S)
        copy(
            feat_ref, feat_all.at[pl.ds(pl.multiple_of(other * R, R), R)],
            s_feat.at[other], r_feat.at[other], (other, d),
        ).wait_recv()

    CH = min(N, 512)
    for layer in range(LINE_LAYERS):
        e = dil_ref[layer]
        for first in range(0, N, CH):
            if layer == 0:
                h = feat_all[first : first + CH, :].astype(F32)
            else:
                h = h1[first : first + CH, :]
            acts[layer, HALO + first : HALO + first + CH, :] = rounded(gelu_pair(h)[0])
        for first in range(0, N, CH):
            taps = [
                acts[layer, pl.ds(HALO + first + (t - 1) * e, CH), :].astype(BF16)
                for t in range(3)
            ]
            total = dot(taps[0], w1_ref[layer, 0])
            total = total + dot(taps[1], w1_ref[layer, 1])
            total = total + dot(taps[2], w1_ref[layer, 2])
            if layer == 0:
                h1[first : first + CH, :] = rounded(
                    feat_all[first : first + CH, :].astype(F32) + total
                )
            else:
                hid[HOFF + first : HOFF + first + CH, :] = rounded(
                    h1[first : first + CH, :] + total
                )

    for a, b in neighbours:
        @pl.when(exists(a, b))
        def _():
            copy(
                maskt.at[1, 1], maskt.at[1 + a, 1 + b],
                s_mask.at[1 + a, 1 + b], r_mask.at[1 + a, 1 + b], (s + a, d + b),
            ).wait_recv()

    for a in range(3):
        mrow[a, 0:8, :] = maskt[a, 0, 8:16, :]
        mrow[a, 8 : 8 + B // 2, :] = jnp.broadcast_to(maskt[a, 1, 0:1, :], (B // 2, C))
        mrow[a, 8 + B // 2 : 8 + B, :] = jnp.broadcast_to(maskt[a, 1, 8:9, :], (B // 2, C))
        mrow[a, 8 + B : 16 + B, :] = maskt[a, 2, 0:8, :]

    WIDE = B + 2 * HALO

    def band_row(li, kind):
        start = HOFF + row0 - HALO + li
        own = hid[pl.ds(start, 1), :]
        partner = hid[pl.ds(start + d0 - HALO, WIDE), :]
        return rounded(mrow[kind] * 0.5 * (own + partner))

    def spread(target, li, direction):
        for tap in range(3):
            piece = wide[li, pl.ds(HALO + direction * (tap - 1) * e2, B), :]
            target[li, :, tap * C : (tap + 1) * C] = piece.astype(BF16)

    def inner_row(li):
        v = band_row(li, 1)
        value, half = gelu_pair(v)
        wide[li] = rounded(value)
        mid = slice(HALO, HALO + B)
        slope[li - HALO] = slope_from(v[mid], half[mid])
        bandin[li - HALO] = v[mid].astype(BF16)
        spread(p3, li, 1)

    pl.loop(HALO, HALO + R)(inner_row)

    @pl.loop(0, 2 * HALO)
    def _(index):
        low = (index < HALO).astype(jnp.int32)
        li = index + (1 - low) * R
        wide[li] = rounded(gelu_pair(band_row(li, 2 * (1 - low)))[0])
        spread(p3, li, 1)

    for a, b in neighbours:
        @pl.when(exists(a, b))
        def _():
            copy(
                halo_slot(a, b), halo_slot(a, b),
                s_halo.at[1 + a, 1 + b], r_halo.at[1 + a, 1 + b], (s + a, d + b),
            ).wait_recv()

    def gm_row(li, kind, lo, mid, hi):
        wide[li, 0:HALO, :] = mrow[kind, 0:HALO, :] * lo.astype(F32)[8:16]
        wide[li, HALO : HALO + B, :] = mrow[kind, HALO : HALO + B, :] * mid.astype(F32)
        wide[li, HALO + B :, :] = mrow[kind, HALO + B :, :] * hi.astype(F32)[0:8]
        spread(g3, li, -1)

    @pl.loop(0, R)
    def _(i):
        gm_row(i + HALO, 1, left[i], grad_ref[i], right[i])

    @pl.loop(0, HALO)
    def _(i):
        gm_row(i, 0, corner[0, 0, i], top[i], corner[0, 1, i])
        gm_row(i + HALO + R, 2, corner[1, 0, i], bottom[i], corner[1, 1, i])

    KR = 8

    @pl.loop(0, R // KR)
    def _(step):
        i0 = HALO + step * KR
        gm = g3[pl.ds(i0, KR), :, C : 2 * C].reshape(KR * B, C)
        for a in range(3):
            pa = p3[pl.ds(i0 + (a - 1) * e2, KR)].reshape(KR * B, 3 * C)
            wg[a] += dot(gm, pa, ((0,), (0,)))

    for a in range(3):
        for b in range(3):
            wsend[(3 * a + b) * C : (3 * a + b + 1) * C, :] = (
                wg[a, :, b * C : (b + 1) * C].T.astype(BF16)
            )

    def piece_at(owner):
        return pl.ds(pl.multiple_of(owner * PIECE, 16), PIECE)

    def ws_copy(owner, sender):
        return copy(
            wsend.at[piece_at(owner)], wrecv.at[sender],
            s_ws.at[owner], r_ws.at[sender], device(owner),
        )

    @pl.loop(0, NOWN)
    def _(owner):
        @pl.when(owner != me)
        def _():
            ws_copy(owner, me).start()

    @pl.when(me < NOWN)
    def _():
        wrecv[me] = wsend[piece_at(me), :]

    RR = 4

    @pl.loop(0, R // RR)
    def _(step):
        i0 = step * RR
        taps = [g3[pl.ds(HALO + i0 - (a - 1) * e2, RR)].reshape(RR * B, 3 * C) for a in range(3)]
        r = dot(taps[0], w2t[0]) + dot(taps[1], w2t[1]) + dot(taps[2], w2t[2])
        r = r.reshape(RR, B, C)
        for k in range(RR):
            gm = g3[HALO + i0 + k, :, C : 2 * C].astype(F32)
            m = mrow[1, HALO : HALO + B, :]
            u = rounded(0.5 * m * (gm + slope[i0 + k] * r[k]))
            rowpart[pl.ds(i0 + k, 1), :] = jnp.sum(u, axis=0, keepdims=True)
            colpart[pl.ds(i0 + k, B), :] += u

    PARTS = RATIO + 1

    def g_move(source, slot, target, quarter, index, action):
        dev_is_me = (target == s) & (quarter == d)

        @pl.when((target < S) & jnp.logical_not(dev_is_me))
        def _():
            c = copy(source, gslots.at[slot], s_g.at[index], r_g.at[slot], (target, quarter))
            c.start() if action == "start" else c.wait_send()

        if action == "start":
            @pl.when(dev_is_me)
            def _():
                gslots[slot] = source[...]

    def g_all(action):
        for quarter in range(D):
            g_move(
                rowpart.at[pl.ds(quarter * Q, Q)], d, s, quarter, quarter, action
            )
            for k in range(PARTS):
                g_move(
                    colpart.at[pl.ds(k * R + quarter * Q, Q)],
                    D + d * PARTS + k, s + d * RATIO + k, quarter,
                    D + quarter * PARTS + k, action,
                )

    g_all("start")

    @pl.loop(0, R // RR)
    def _(step):
        i0 = step * RR
        taps = [p3[pl.ds(HALO + i0 + (a - 1) * e2, RR)].reshape(RR * B, 3 * C) for a in range(3)]
        q = dot(taps[0], w2_ref[0].reshape(3 * C, C))
        q = q + dot(taps[1], w2_ref[1].reshape(3 * C, C))
        q = q + dot(taps[2], w2_ref[2].reshape(3 * C, C))
        q = q.reshape(RR, B, C)
        for k in range(RR):
            m = mrow[1, HALO : HALO + B, :]
            out_ref[i0 + k] = (m * (bandin[i0 + k].astype(F32) + q[k])).astype(BF16)

    for diag in range(D):
        @pl.when(d != diag)
        def _():
            copy(gmine, gslots.at[diag], s_g.at[0], r_g.at[diag], (s, diag)).wait_recv()

        for k in range(PARTS):
            slot = D + diag * PARTS + k
            source = s - diag * RATIO - k
            remote = (source >= 0) & jnp.logical_not((source == s) & (d == diag))

            @pl.when(remote)
            def _():
                copy(gmine, gslots.at[slot], s_g.at[0], r_g.at[slot], (source, diag)).wait_recv()

            @pl.when(source < 0)
            def _():
                gslots[slot] = jnp.zeros((Q, C), F32)

    gmine[...] = jnp.sum(gslots[...], axis=0)

    def ga_copy(other, sender):
        return copy(
            gmine, gall.at[pl.ds(pl.multiple_of(sender * Q, Q), Q)],
            s_ga.at[other], r_ga.at[sender], device(other),
        )

    @pl.loop(1, NDEV)
    def _(step):
        ga_copy(lax.rem(me + step, NDEV), me).start()

    gall[pl.ds(pl.multiple_of(me * Q, Q), Q), :] = gmine[...]

    scaling = 1.0 / math.sqrt(N)

    def wa_copy(other, owner):
        return copy(
            wsum, wall.at[piece_at(owner)], s_wa.at[other], r_wa.at[owner], device(other)
        )

    @pl.when(me < NOWN)
    def _():
        @pl.loop(1, NDEV)
        def _(step):
            other = lax.rem(me + step, NDEV)
            ws_copy(me, other).wait_recv()

        total = wrecv[0].astype(F32)
        for k in range(1, NDEV):
            total = total + wrecv[k].astype(F32)
        wsum[...] = (total * scaling).astype(BF16)

        @pl.loop(1, NDEV)
        def _(step):
            wa_copy(lax.rem(me + step, NDEV), me).start()

        wall[piece_at(me), :] = wsum[...]

    @pl.loop(1, NDEV)
    def _(step):
        other = lax.rem(me + step, NDEV)
        ga_copy(other, other).wait_recv()

    for layer in reversed(range(LINE_LAYERS)):
        e = dil_ref[layer]
        for first in range(0, N, CH):
            gpad[HALO + first : HALO + first + CH, :] = rounded(gall[first : first + CH, :])
        for t in range(3):
            total = None
            for first in range(0, N, CH):
                tap = acts[layer, pl.ds(HALO + first + (t - 1) * e, CH), :].astype(BF16)
                gb = gpad[HALO + first : HALO + first + CH, :].astype(BF16)
                term = dot(tap, gb, ((0,), (0,)))
                total = term if total is None else total + term
            c1_ref[layer, t] = total * scaling
        for first in range(0, N, CH):
            total = None
            for t in range(3):
                tap = gpad[pl.ds(HALO + first - (t - 1) * e, CH), :].astype(BF16)
                term = dot(tap, w1_ref[layer, t], ((1,), (1,)))
                total = term if total is None else total + term
            if layer == 0:
                h = feat_all[first : first + CH, :].astype(F32)
            else:
                h = h1[first : first + CH, :]
            gall[first : first + CH, :] += slope_from(h, gelu_pair(h)[1]) * total
    seqg_ref[...] = gall[pl.ds(pl.multiple_of(row0, R), R), :]

    @pl.loop(0, NOWN)
    def _(owner):
        @pl.when(owner != me)
        def _():
            wa_copy(me, owner).wait_recv()

    c2_ref[...] = wall[...].astype(F32)

    @pl.loop(1, S)
    def _(step):
        feat_copy(lax.rem(s + step, S)).wait_send()

    for a, b in neighbours:
        @pl.when(exists(a, b))
        def _():
            mask_copy(a, b).wait_send()
            halo_copy(a, b).wait_send()

    g_all("wait")

    @pl.loop(0, NOWN)
    def _(owner):
        @pl.when(owner != me)
        def _():
            ws_copy(owner, me).wait_send()

    @pl.loop(1, NDEV)
    def _(step):
        other = lax.rem(me + step, NDEV)
        ga_copy(other, me).wait_send()

        @pl.when(me < NOWN)
        def _():
            wa_copy(other, me).wait_send()


def body(seq_feat, conv1_weight, conv2_kernel_weight, dilations, block_mask, band_grad):
    S = lax.axis_size("seq")
    D = lax.axis_size("diag")
    R, C = seq_feat.shape
    B = band_grad.shape[1]
    N = R * S
    W = B * D
    NDEV = S * D
    NOWN = owners_for(9 * C // 16, NDEV)
    PIECE = 9 * C // NOWN
    PARTS = B // R + 1
    Q = R // D
    RH, WIDE = R + 2 * HALO, B + 2 * HALO
    vmem = pl.BlockSpec(memory_space=pltpu.VMEM)
    smem = pl.BlockSpec(memory_space=pltpu.SMEM)
    dma = pltpu.SemaphoreType.DMA
    scratch = [
        pltpu.VMEM((N, C), BF16),
        pltpu.VMEM((HOFF + N + W + 32, C), F32),
        pltpu.VMEM((N, C), F32),
        pltpu.VMEM((LINE_LAYERS, N + 2 * HALO, C), F32),
        pltpu.VMEM((3, 3, 16, C), F32),
        pltpu.VMEM((3, WIDE, C), F32),
        pltpu.VMEM((RH, WIDE, C), F32),
        pltpu.VMEM((RH, B, 3 * C), BF16),
        pltpu.VMEM((RH, B, 3 * C), BF16),
        pltpu.VMEM((R, B, C), F32),
        pltpu.VMEM((R, B, C), BF16),
        pltpu.VMEM((3, 3 * C, C), BF16),
        pltpu.VMEM((HALO, B, C), BF16),
        pltpu.VMEM((HALO, B, C), BF16),
        pltpu.VMEM((R, 16, C), BF16),
        pltpu.VMEM((R, 16, C), BF16),
        pltpu.VMEM((2, 2, HALO, 16, C), BF16),
        pltpu.VMEM((3, C, 3 * C), F32),
        pltpu.VMEM((9 * C, C), BF16),
        pltpu.VMEM((NDEV, PIECE, C), BF16),
        pltpu.VMEM((PIECE, C), BF16),
        pltpu.VMEM((9 * C, C), BF16),
        pltpu.VMEM((R, C), F32),
        pltpu.VMEM((R + B, C), F32),
        pltpu.VMEM((D + D * PARTS, Q, C), F32),
        pltpu.VMEM((Q, C), F32),
        pltpu.VMEM((N, C), F32),
        pltpu.VMEM((N + 2 * HALO, C), F32),
        dma((S,)), dma((S,)),
        dma((3, 3)), dma((3, 3)),
        dma((3, 3)), dma((3, 3)),
        dma((NDEV,)), dma((NDEV,)),
        dma((NDEV,)), dma((NDEV,)),
        dma((D + D * PARTS,)), dma((D + D * PARTS,)),
        dma((NDEV,)), dma((NDEV,)),
    ]
    band_out, seq_grad, conv1_grad, conv2_grad = pl.pallas_call(
        functools.partial(kernel, S, D, R, B, C, NOWN),
        out_shape=(
            jax.ShapeDtypeStruct((R, B, C), BF16),
            jax.ShapeDtypeStruct((R, C), F32),
            jax.ShapeDtypeStruct((LINE_LAYERS, 3, C, C), F32),
            jax.ShapeDtypeStruct((9 * C, C), F32),
        ),
        in_specs=[vmem, vmem, vmem, smem, smem, vmem],
        out_specs=(vmem, vmem, vmem, vmem),
        scratch_shapes=scratch,
        compiler_params=pltpu.CompilerParams(
            collective_id=0, has_side_effects=True, vmem_limit_bytes=58 * 1024 * 1024
        ),
        name="section",
    )(seq_feat, conv1_weight, conv2_kernel_weight, dilations, block_mask, band_grad)
    return band_out, seq_grad, conv1_grad, conv2_grad.reshape(3, 3, C, C)


def solution(mesh):
    return jax.shard_map(
        body,
        mesh=mesh,
        in_specs=(P("seq", None), P(), P(), P(), P("seq", "diag"), P("seq", "diag", None)),
        out_specs=(P("seq", "diag", None), P("seq", None), P(), P()),
        check_vma=False,
    )
```

```python
import functools
import math

import jax
import jax.numpy as jnp
from jax import lax
from jax.experimental import pallas as pl
from jax.experimental.pallas import tpu as pltpu
from jax.sharding import PartitionSpec as P

BLOCK = 64
HALO = 8
LINE_LAYERS = 2
HOFF = 16
MESH = pl.DeviceIdType.MESH

root_half = 0.7071067811865476
inv_root_two_pi = 0.3989422804014327

F32 = jnp.float32
BF16 = jnp.bfloat16


def rounded(x):
    return x.astype(BF16).astype(F32)


def gelu_pair(v):
    half = 0.5 * (1.0 + lax.erf(v * root_half))
    return v * half, half


def slope_from(v, half):
    return half + v * jnp.exp(-0.5 * v * v) * inv_root_two_pi


def dot(a, b, dims=((1,), (0,))):
    return lax.dot_general(a, b, (dims, ((), ())), preferred_element_type=F32)


def owners_for(units, devices):
    return max(n for n in range(1, devices + 1) if units % n == 0)


def kernel(
    S, D, R, B, C, NOWN,
    feat_ref, w1_ref, w2_ref, dil_ref, mask_ref, grad_ref,
    out_ref, seqg_ref, c1_ref, c2_ref,
    feat_all, hid, h1, acts, maskt, mrow, wide, p3, g3, slope, bandin, w2t,
    top, bottom, left, right, corner,
    wg, wsend, wrecv, wsum, wall, rowpart, colpart, gslots, gmine, gall, gpad, gallb, out_scr,
    s_feat, r_feat, s_halo, r_halo, s_mask, r_mask, s_ws, r_ws, s_wa, r_wa,
    s_g, r_g, s_ga, r_ga, s_out,
):
    N = R * S
    W = B * D
    NDEV = S * D
    PIECE = 9 * C // NOWN
    RATIO = B // R
    Q = R // D
    s = lax.axis_index("seq")
    d = lax.axis_index("diag")
    me = s * D + d
    row0 = s * R
    d0 = d * B
    e2 = dil_ref[LINE_LAYERS]

    def device(index):
        return (index // D, index % D)

    def copy(src, dst, ss, rs, dev):
        return pltpu.make_async_remote_copy(
            src_ref=src, dst_ref=dst, send_sem=ss, recv_sem=rs,
            device_id=dev, device_id_type=MESH,
        )

    for k in range(2):
        value = mask_ref[0, k].astype(F32)
        maskt[1, 1, 8 * k : 8 * k + 8, :] = jnp.full((8, C), 1.0, F32) * value

    barrier = pltpu.get_barrier_semaphore()

    @pl.loop(1, NDEV)
    def _(step):
        pl.semaphore_signal(
            barrier, inc=1, device_id=device(lax.rem(me + step, NDEV)), device_id_type=MESH
        )

    pl.semaphore_wait(barrier, NDEV - 1)

    def feat_copy(other):
        return copy(
            feat_ref, feat_all.at[pl.ds(pl.multiple_of(row0, R), R)],
            s_feat.at[other], r_feat.at[s], (other, d),
        )

    @pl.loop(1, S)
    def _(step):
        feat_copy(lax.rem(s + step, S)).start()

    neighbours = [(a, b) for a in (-1, 0, 1) for b in (-1, 0, 1) if (a, b) != (0, 0)]

    def exists(a, b):
        return (s + a >= 0) & (s + a < S) & (d + b >= 0) & (d + b < D)

    def mask_copy(a, b):
        return copy(
            maskt.at[1, 1], maskt.at[1 - a, 1 - b],
            s_mask.at[1 + a, 1 + b], r_mask.at[1 - a, 1 - b], (s + a, d + b),
        )

    def halo_slot(a, b):
        if b == 0:
            return top if a < 0 else bottom
        if a == 0:
            return left if b < 0 else right
        return corner.at[(1 + a) // 2, (1 + b) // 2]

    def halo_copy(a, b):
        rows = {-1: pl.ds(0, HALO), 0: pl.ds(0, R), 1: pl.ds(R - HALO, HALO)}[a]
        cols = {-1: pl.ds(0, 16), 0: pl.ds(0, B), 1: pl.ds(B - 16, 16)}[b]
        return copy(
            grad_ref.at[rows, cols], halo_slot(-a, -b),
            s_halo.at[1 + a, 1 + b], r_halo.at[1 - a, 1 - b], (s + a, d + b),
        )

    for a, b in neighbours:
        @pl.when(exists(a, b))
        def _():
            mask_copy(a, b).start()

    sides = [(0, -1), (0, 1)]
    edges = [(-1, 0), (1, 0), (-1, -1), (-1, 1), (1, -1), (1, 1)]
    for a, b in sides + edges:
        @pl.when(exists(a, b))
        def _():
            halo_copy(a, b).start()

        @pl.when(jnp.logical_not(exists(a, b)))
        def _():
            maskt[1 + a, 1 + b] = jnp.zeros((16, C), F32)
            slot = halo_slot(a, b)
            slot[...] = jnp.zeros(slot.shape, BF16)

    feat_all[pl.ds(pl.multiple_of(row0, R), R), :] = feat_ref[...]
    hid[0:HOFF, :] = jnp.zeros((HOFF, C), F32)
    hid[HOFF + N :, :] = jnp.zeros((hid.shape[0] - HOFF - N, C), F32)
    for layer in range(LINE_LAYERS):
        acts[layer, 0:HALO, :] = jnp.zeros((HALO, C), F32)
        acts[layer, HALO + N :, :] = jnp.zeros((HALO, C), F32)
    gpad[0:HALO, :] = jnp.zeros((HALO, C), F32)
    gpad[HALO + N :, :] = jnp.zeros((HALO, C), F32)
    for a in range(3):
        for b in range(3):
            w2t[a, b * C : (b + 1) * C, :] = w2_ref[a, b].astype(F32).T.astype(BF16)
    wg[...] = jnp.zeros(wg.shape, F32)
    colpart[...] = jnp.zeros(colpart.shape, F32)

    @pl.loop(1, S)
    def _(step):
        other = lax.rem(s + step, S)
        copy(
            feat_ref, feat_all.at[pl.ds(pl.multiple_of(other * R, R), R)],
            s_feat.at[other], r_feat.at[other], (other, d),
        ).wait_recv()

    CH = min(N, 512)
    for layer in range(LINE_LAYERS):
        e = dil_ref[layer]
        for first in range(0, N, CH):
            if layer == 0:
                h = feat_all[first : first + CH, :].astype(F32)
            else:
                h = h1[first : first + CH, :]
            acts[layer, HALO + first : HALO + first + CH, :] = rounded(gelu_pair(h)[0])
        for first in range(0, N, CH):
            taps = [
                acts[layer, pl.ds(HALO + first + (t - 1) * e, CH), :].astype(BF16)
                for t in range(3)
            ]
            total = dot(taps[0], w1_ref[layer, 0])
            total = total + dot(taps[1], w1_ref[layer, 1])
            total = total + dot(taps[2], w1_ref[layer, 2])
            if layer == 0:
                h1[first : first + CH, :] = rounded(
                    feat_all[first : first + CH, :].astype(F32) + total
                )
            else:
                hid[HOFF + first : HOFF + first + CH, :] = rounded(
                    h1[first : first + CH, :] + total
                )

    for a, b in neighbours:
        @pl.when(exists(a, b))
        def _():
            copy(
                maskt.at[1, 1], maskt.at[1 + a, 1 + b],
                s_mask.at[1 + a, 1 + b], r_mask.at[1 + a, 1 + b], (s + a, d + b),
            ).wait_recv()

    for a in range(3):
        mrow[a, 0:8, :] = maskt[a, 0, 8:16, :]
        mrow[a, 8 : 8 + B // 2, :] = jnp.broadcast_to(maskt[a, 1, 0:1, :], (B // 2, C))
        mrow[a, 8 + B // 2 : 8 + B, :] = jnp.broadcast_to(maskt[a, 1, 8:9, :], (B // 2, C))
        mrow[a, 8 + B : 16 + B, :] = maskt[a, 2, 0:8, :]

    WIDE = B + 2 * HALO

    def band_row(li, kind):
        start = HOFF + row0 - HALO + li
        own = hid[pl.ds(start, 1), :]
        partner = hid[pl.ds(start + d0 - HALO, WIDE), :]
        return rounded(mrow[kind] * 0.5 * (own + partner))

    def spread(target, li, direction):
        for tap in range(3):
            piece = wide[li, pl.ds(HALO + direction * (tap - 1) * e2, B), :]
            target[li, :, tap * C : (tap + 1) * C] = piece.astype(BF16)

    def inner_row(li):
        v = band_row(li, 1)
        value, half = gelu_pair(v)
        wide[li] = rounded(value)
        mid = slice(HALO, HALO + B)
        slope[li - HALO] = slope_from(v[mid], half[mid])
        bandin[li - HALO] = v[mid].astype(BF16)
        spread(p3, li, 1)

    pl.loop(HALO, HALO + R)(inner_row)

    @pl.loop(0, 2 * HALO)
    def _(index):
        low = (index < HALO).astype(jnp.int32)
        li = index + (1 - low) * R
        wide[li] = rounded(gelu_pair(band_row(li, 2 * (1 - low)))[0])
        spread(p3, li, 1)

    def wait_halos(which):
        for a, b in which:
            @pl.when(exists(a, b))
            def _():
                copy(
                    halo_slot(a, b), halo_slot(a, b),
                    s_halo.at[1 + a, 1 + b], r_halo.at[1 + a, 1 + b], (s + a, d + b),
                ).wait_recv()

    wait_halos(sides)

    def gm_row(li, kind, lo, mid, hi):
        wide[li, 0:HALO, :] = mrow[kind, 0:HALO, :] * lo.astype(F32)[8:16]
        wide[li, HALO : HALO + B, :] = mrow[kind, HALO : HALO + B, :] * mid.astype(F32)
        wide[li, HALO + B :, :] = mrow[kind, HALO + B :, :] * hi.astype(F32)[0:8]
        spread(g3, li, -1)

    @pl.loop(0, R)
    def _(i):
        gm_row(i + HALO, 1, left[i], grad_ref[i], right[i])

    KR = 8

    @pl.loop(0, R // KR)
    def _(step):
        i0 = HALO + step * KR
        gm = g3[pl.ds(i0, KR), :, C : 2 * C].reshape(KR * B, C)
        for a in range(3):
            pa = p3[pl.ds(i0 + (a - 1) * e2, KR)].reshape(KR * B, 3 * C)
            wg[a] += dot(gm, pa, ((0,), (0,)))

    for a in range(3):
        for b in range(3):
            wsend[(3 * a + b) * C : (3 * a + b + 1) * C, :] = (
                wg[a, :, b * C : (b + 1) * C].T.astype(BF16)
            )

    def piece_at(owner):
        return pl.ds(pl.multiple_of(owner * PIECE, 16), PIECE)

    def ws_copy(owner, sender):
        return copy(
            wsend.at[piece_at(owner)], wrecv.at[sender],
            s_ws.at[owner], r_ws.at[sender], device(owner),
        )

    @pl.loop(0, NOWN)
    def _(owner):
        @pl.when(owner != me)
        def _():
            ws_copy(owner, me).start()

    @pl.when(me < NOWN)
    def _():
        wrecv[me] = wsend[piece_at(me), :]

    RR = 4

    def back_rows(step):
        i0 = step * RR
        taps = [g3[pl.ds(HALO + i0 - (a - 1) * e2, RR)].reshape(RR * B, 3 * C) for a in range(3)]
        r = dot(taps[0], w2t[0]) + dot(taps[1], w2t[1]) + dot(taps[2], w2t[2])
        r = r.reshape(RR, B, C)
        for k in range(RR):
            gm = g3[HALO + i0 + k, :, C : 2 * C].astype(F32)
            m = mrow[1, HALO : HALO + B, :]
            u = rounded(0.5 * m * (gm + slope[i0 + k] * r[k]))
            rowpart[pl.ds(i0 + k, 1), :] = jnp.sum(u, axis=0, keepdims=True)
            colpart[pl.ds(i0 + k, B), :] += u

    pl.loop(HALO // RR, (R - HALO) // RR)(back_rows)
    wait_halos(edges)

    @pl.loop(0, HALO)
    def _(i):
        gm_row(i, 0, corner[0, 0, i], top[i], corner[0, 1, i])
        gm_row(i + HALO + R, 2, corner[1, 0, i], bottom[i], corner[1, 1, i])

    pl.loop(0, HALO // RR)(back_rows)
    pl.loop((R - HALO) // RR, R // RR)(back_rows)

    PARTS = RATIO + 1

    def g_move(source, slot, target, quarter, index, action):
        dev_is_me = (target == s) & (quarter == d)

        @pl.when((target < S) & jnp.logical_not(dev_is_me))
        def _():
            c = copy(source, gslots.at[slot], s_g.at[index], r_g.at[slot], (target, quarter))
            c.start() if action == "start" else c.wait_send()

        if action == "start":
            @pl.when(dev_is_me)
            def _():
                gslots[slot] = source[...]

    def g_all(action):
        for quarter in range(D):
            g_move(
                rowpart.at[pl.ds(quarter * Q, Q)], d, s, quarter, quarter, action
            )
            for k in range(PARTS):
                g_move(
                    colpart.at[pl.ds(k * R + quarter * Q, Q)],
                    D + d * PARTS + k, s + d * RATIO + k, quarter,
                    D + quarter * PARTS + k, action,
                )

    g_all("start")

    @pl.loop(0, R // RR)
    def _(step):
        i0 = step * RR
        taps = [p3[pl.ds(HALO + i0 + (a - 1) * e2, RR)].reshape(RR * B, 3 * C) for a in range(3)]
        q = dot(taps[0], w2_ref[0].reshape(3 * C, C))
        q = q + dot(taps[1], w2_ref[1].reshape(3 * C, C))
        q = q + dot(taps[2], w2_ref[2].reshape(3 * C, C))
        q = q.reshape(RR, B, C)
        for k in range(RR):
            m = mrow[1, HALO : HALO + B, :]
            out_scr[i0 + k] = (m * (bandin[i0 + k].astype(F32) + q[k])).astype(BF16)

    out_copy = pltpu.make_async_copy(out_scr, out_ref, s_out)
    out_copy.start()

    for diag in range(D):
        @pl.when(d != diag)
        def _():
            copy(rowpart.at[pl.ds(0, Q)], gslots.at[diag], s_g.at[0], r_g.at[diag], (s, diag)).wait_recv()

        for k in range(PARTS):
            slot = D + diag * PARTS + k
            source = s - diag * RATIO - k
            remote = (source >= 0) & jnp.logical_not((source == s) & (d == diag))

            @pl.when(remote)
            def _():
                copy(rowpart.at[pl.ds(0, Q)], gslots.at[slot], s_g.at[0], r_g.at[slot], (source, diag)).wait_recv()

            @pl.when(source < 0)
            def _():
                gslots[slot] = jnp.zeros((Q, C), F32)

    gmine[...] = jnp.sum(gslots[...], axis=0).astype(BF16)

    def ga_copy(other, sender):
        return copy(
            gmine, gallb.at[pl.ds(pl.multiple_of(sender * Q, Q), Q)],
            s_ga.at[other], r_ga.at[sender], device(other),
        )

    @pl.loop(1, NDEV)
    def _(step):
        ga_copy(lax.rem(me + step, NDEV), me).start()

    gallb[pl.ds(pl.multiple_of(me * Q, Q), Q), :] = gmine[...]

    scaling = 1.0 / math.sqrt(N)

    def wa_copy(other, owner):
        return copy(
            wsum, wall.at[piece_at(owner)], s_wa.at[other], r_wa.at[owner], device(other)
        )

    @pl.when(me < NOWN)
    def _():
        @pl.loop(1, NDEV)
        def _(step):
            other = lax.rem(me + step, NDEV)
            ws_copy(me, other).wait_recv()

        total = wrecv[0].astype(F32)
        for k in range(1, NDEV):
            total = total + wrecv[k].astype(F32)
        wsum[...] = (total * scaling).astype(BF16)

        @pl.loop(1, NDEV)
        def _(step):
            wa_copy(lax.rem(me + step, NDEV), me).start()

        wall[piece_at(me), :] = wsum[...]

    @pl.loop(1, NDEV)
    def _(step):
        other = lax.rem(me + step, NDEV)
        ga_copy(other, other).wait_recv()

    gall[...] = gallb[...].astype(F32)

    for layer in reversed(range(LINE_LAYERS)):
        e = dil_ref[layer]
        for first in range(0, N, CH):
            gpad[HALO + first : HALO + first + CH, :] = rounded(gall[first : first + CH, :])
        for t in range(3):
            total = None
            for first in range(0, N, CH):
                tap = acts[layer, pl.ds(HALO + first + (t - 1) * e, CH), :].astype(BF16)
                gb = gpad[HALO + first : HALO + first + CH, :].astype(BF16)
                term = dot(tap, gb, ((0,), (0,)))
                total = term if total is None else total + term
            c1_ref[layer, t] = total * scaling
        for first in range(0, N, CH):
            total = None
            for t in range(3):
                tap = gpad[pl.ds(HALO + first - (t - 1) * e, CH), :].astype(BF16)
                term = dot(tap, w1_ref[layer, t], ((1,), (1,)))
                total = term if total is None else total + term
            if layer == 0:
                h = feat_all[first : first + CH, :].astype(F32)
            else:
                h = h1[first : first + CH, :]
            gall[first : first + CH, :] += slope_from(h, gelu_pair(h)[1]) * total
    seqg_ref[...] = gall[pl.ds(pl.multiple_of(row0, R), R), :]

    @pl.loop(0, NOWN)
    def _(owner):
        @pl.when(owner != me)
        def _():
            wa_copy(me, owner).wait_recv()

    c2_ref[...] = wall[...].astype(F32)

    out_copy.wait()

    @pl.loop(1, S)
    def _(step):
        feat_copy(lax.rem(s + step, S)).wait_send()

    for a, b in neighbours:
        @pl.when(exists(a, b))
        def _():
            mask_copy(a, b).wait_send()
            halo_copy(a, b).wait_send()

    g_all("wait")

    @pl.loop(0, NOWN)
    def _(owner):
        @pl.when(owner != me)
        def _():
            ws_copy(owner, me).wait_send()

    @pl.loop(1, NDEV)
    def _(step):
        other = lax.rem(me + step, NDEV)
        ga_copy(other, me).wait_send()

        @pl.when(me < NOWN)
        def _():
            wa_copy(other, me).wait_send()


def place(parts, *refs):
    count = len(parts)
    sources, targets, sems = refs[:count], refs[count : 2 * count], refs[2 * count]
    copies = []
    for source, target, pieces in zip(sources, targets, parts):
        size = source.shape[0] // pieces
        for k in range(pieces):
            rows = pl.ds(k * size, size)
            copies.append(
                pltpu.make_async_copy(source.at[rows], target.at[rows], sems.at[len(copies)])
            )
    for c in copies:
        c.start()
    for c in copies:
        c.wait()


def body(seq_feat, conv1_weight, conv2_kernel_weight, dilations, block_mask, band_grad):
    S = lax.axis_size("seq")
    D = lax.axis_size("diag")
    R, C = seq_feat.shape
    B = band_grad.shape[1]
    N = R * S
    W = B * D
    NDEV = S * D
    NOWN = owners_for(9 * C // 16, NDEV)
    PIECE = 9 * C // NOWN
    PARTS = B // R + 1
    Q = R // D
    RH, WIDE = R + 2 * HALO, B + 2 * HALO
    vmem = pl.BlockSpec(memory_space=pltpu.VMEM)
    smem = pl.BlockSpec(memory_space=pltpu.SMEM)
    dma = pltpu.SemaphoreType.DMA
    scratch = [
        pltpu.VMEM((N, C), BF16),
        pltpu.VMEM((HOFF + N + W + 32, C), F32),
        pltpu.VMEM((N, C), F32),
        pltpu.VMEM((LINE_LAYERS, N + 2 * HALO, C), F32),
        pltpu.VMEM((3, 3, 16, C), F32),
        pltpu.VMEM((3, WIDE, C), F32),
        pltpu.VMEM((RH, WIDE, C), F32),
        pltpu.VMEM((RH, B, 3 * C), BF16),
        pltpu.VMEM((RH, B, 3 * C), BF16),
        pltpu.VMEM((R, B, C), F32),
        pltpu.VMEM((R, B, C), BF16),
        pltpu.VMEM((3, 3 * C, C), BF16),
        pltpu.VMEM((HALO, B, C), BF16),
        pltpu.VMEM((HALO, B, C), BF16),
        pltpu.VMEM((R, 16, C), BF16),
        pltpu.VMEM((R, 16, C), BF16),
        pltpu.VMEM((2, 2, HALO, 16, C), BF16),
        pltpu.VMEM((3, C, 3 * C), F32),
        pltpu.VMEM((9 * C, C), BF16),
        pltpu.VMEM((NDEV, PIECE, C), BF16),
        pltpu.VMEM((PIECE, C), BF16),
        pltpu.VMEM((9 * C, C), BF16),
        pltpu.VMEM((R, C), F32),
        pltpu.VMEM((R + B, C), F32),
        pltpu.VMEM((D + D * PARTS, Q, C), F32),
        pltpu.VMEM((Q, C), BF16),
        pltpu.VMEM((N, C), F32),
        pltpu.VMEM((N + 2 * HALO, C), F32),
        pltpu.VMEM((N, C), BF16),
        pltpu.VMEM((R, B, C), BF16),
        dma((S,)), dma((S,)),
        dma((3, 3)), dma((3, 3)),
        dma((3, 3)), dma((3, 3)),
        dma((NDEV,)), dma((NDEV,)),
        dma((NDEV,)), dma((NDEV,)),
        dma((D + D * PARTS,)), dma((D + D * PARTS,)),
        dma((NDEV,)), dma((NDEV,)), dma,
    ]
    band_out, seq_grad, conv1_grad, conv2_grad = pl.pallas_call(
        functools.partial(kernel, S, D, R, B, C, NOWN),
        out_shape=(
            jax.ShapeDtypeStruct((R, B, C), BF16),
            jax.ShapeDtypeStruct((R, C), F32),
            jax.ShapeDtypeStruct((LINE_LAYERS, 3, C, C), F32),
            jax.ShapeDtypeStruct((9 * C, C), F32),
        ),
        in_specs=[vmem, vmem, vmem, smem, smem, vmem],
        out_specs=(pl.BlockSpec(memory_space=pl.ANY), vmem, vmem, vmem),
        scratch_shapes=scratch,
        compiler_params=pltpu.CompilerParams(
            collective_id=0, has_side_effects=True, vmem_limit_bytes=min(58 << 20, (48 << 20) + 28 * N * C)
        ),
        name="section",
    )(seq_feat, conv1_weight, conv2_kernel_weight, dilations, block_mask, band_grad)
    results = (band_out, seq_grad, conv1_grad, conv2_grad)
    parts = (8, 1, 2, 3)
    anywhere = pl.BlockSpec(memory_space=pl.ANY)
    band_out, seq_grad, conv1_grad, conv2_grad = pl.pallas_call(
        functools.partial(place, parts),
        out_shape=tuple(jax.ShapeDtypeStruct(x.shape, x.dtype) for x in results),
        in_specs=[anywhere] * 4,
        out_specs=(anywhere,) * 4,
        scratch_shapes=[dma((sum(parts),))],
        compiler_params=pltpu.CompilerParams(vmem_limit_bytes=1024 * 1024),
        name="place",
    )(*results)
    return band_out, seq_grad, conv1_grad, conv2_grad.reshape(3, 3, C, C)


def solution(mesh):
    return jax.shard_map(
        body,
        mesh=mesh,
        in_specs=(P("seq", None), P(), P(), P(), P("seq", "diag"), P("seq", "diag", None)),
        out_specs=(P("seq", "diag", None), P("seq", None), P(), P()),
        check_vma=False,
    )
```

```python
import functools
import math

import jax
import jax.numpy as jnp
from jax import lax
from jax.experimental import pallas as pl
from jax.experimental.pallas import tpu as pltpu
from jax.sharding import PartitionSpec as P

BLOCK = 64
HALO = 8
LINE_LAYERS = 2
HOFF = 16
MESH = pl.DeviceIdType.MESH

root_half = 0.7071067811865476
inv_root_two_pi = 0.3989422804014327

F32 = jnp.float32
BF16 = jnp.bfloat16


def rounded(x):
    return x.astype(BF16).astype(F32)


def gelu_pair(v):
    half = 0.5 * (1.0 + lax.erf(v * root_half))
    return v * half, half


def slope_from(v, half):
    return half + v * jnp.exp(-0.5 * v * v) * inv_root_two_pi


def dot(a, b, dims=((1,), (0,))):
    return lax.dot_general(a, b, (dims, ((), ())), preferred_element_type=F32)


def owners_for(units, devices):
    return max(n for n in range(1, devices + 1) if units % n == 0)


def kernel(
    S, D, R, B, C, NOWN,
    feat_ref, w1_hbm, w2_hbm, dil_hbm, mask_hbm, grad_hbm,
    out_ref, seqg_ref, c1_ref, c2_ref,
    feat_all, hid, h1, acts, maskt, mrow, wide, p3, g3, slope, bandin, w2t,
    top, bottom, left, right, corner,
    wg, wsend, wrecv, wsum, wall, rowpart, colpart, gslots, gmine, gall, gpad, gallb, out_scr,
    w1_ref, w2_ref, dil_ref, mask_ref, grad_ref, s_in,
    s_feat, r_feat, s_halo, r_halo, s_mask, r_mask, s_ws, r_ws, s_wa, r_wa,
    s_g, r_g, s_ga, r_ga, s_out,
):
    N = R * S
    W = B * D
    NDEV = S * D
    PIECE = 9 * C // NOWN
    RATIO = B // R
    Q = R // D
    s = lax.axis_index("seq")
    d = lax.axis_index("diag")
    me = s * D + d
    row0 = s * R
    d0 = d * B

    def device(index):
        return (index // D, index % D)

    def copy(src, dst, ss, rs, dev):
        return pltpu.make_async_remote_copy(
            src_ref=src, dst_ref=dst, send_sem=ss, recv_sem=rs,
            device_id=dev, device_id_type=MESH,
        )

    own_rows = feat_all.at[pl.ds(pl.multiple_of(row0, R), R)]
    loads = [
        pltpu.make_async_copy(source, target, s_in.at[k])
        for k, (source, target) in enumerate(
            [
                (mask_hbm, mask_ref), (dil_hbm, dil_ref), (feat_ref, own_rows),
                (w1_hbm, w1_ref), (w2_hbm, w2_ref), (grad_hbm, grad_ref),
            ]
        )
    ]
    for load in loads:
        load.start()

    loads[0].wait()
    loads[1].wait()
    e2 = dil_ref[LINE_LAYERS]
    for k in range(2):
        value = mask_ref[0, k].astype(F32)
        maskt[1, 1, 8 * k : 8 * k + 8, :] = jnp.full((8, C), 1.0, F32) * value

    barrier = pltpu.get_barrier_semaphore()

    @pl.loop(1, NDEV)
    def _(step):
        pl.semaphore_signal(
            barrier, inc=1, device_id=device(lax.rem(me + step, NDEV)), device_id_type=MESH
        )

    pl.semaphore_wait(barrier, NDEV - 1)

    def feat_copy(other):
        return copy(
            feat_ref, feat_all.at[pl.ds(pl.multiple_of(row0, R), R)],
            s_feat.at[other], r_feat.at[s], (other, d),
        )

    @pl.loop(1, S)
    def _(step):
        feat_copy(lax.rem(s + step, S)).start()

    neighbours = [(a, b) for a in (-1, 0, 1) for b in (-1, 0, 1) if (a, b) != (0, 0)]

    def exists(a, b):
        return (s + a >= 0) & (s + a < S) & (d + b >= 0) & (d + b < D)

    def mask_copy(a, b):
        return copy(
            maskt.at[1, 1], maskt.at[1 - a, 1 - b],
            s_mask.at[1 + a, 1 + b], r_mask.at[1 - a, 1 - b], (s + a, d + b),
        )

    def halo_slot(a, b):
        if b == 0:
            return top if a < 0 else bottom
        if a == 0:
            return left if b < 0 else right
        return corner.at[(1 + a) // 2, (1 + b) // 2]

    def halo_copy(a, b):
        rows = {-1: pl.ds(0, HALO), 0: pl.ds(0, R), 1: pl.ds(R - HALO, HALO)}[a]
        cols = {-1: pl.ds(0, 16), 0: pl.ds(0, B), 1: pl.ds(B - 16, 16)}[b]
        return copy(
            grad_hbm.at[rows, cols], halo_slot(-a, -b),
            s_halo.at[1 + a, 1 + b], r_halo.at[1 - a, 1 - b], (s + a, d + b),
        )

    for a, b in neighbours:
        @pl.when(exists(a, b))
        def _():
            mask_copy(a, b).start()

    sides = [(0, -1), (0, 1)]
    edges = [(-1, 0), (1, 0), (-1, -1), (-1, 1), (1, -1), (1, 1)]
    for a, b in sides + edges:
        @pl.when(exists(a, b))
        def _():
            halo_copy(a, b).start()

        @pl.when(jnp.logical_not(exists(a, b)))
        def _():
            maskt[1 + a, 1 + b] = jnp.zeros((16, C), F32)
            slot = halo_slot(a, b)
            slot[...] = jnp.zeros(slot.shape, BF16)

    for load in loads[2:]:
        load.wait()
    hid[0:HOFF, :] = jnp.zeros((HOFF, C), F32)
    hid[HOFF + N :, :] = jnp.zeros((hid.shape[0] - HOFF - N, C), F32)
    for layer in range(LINE_LAYERS):
        acts[layer, 0:HALO, :] = jnp.zeros((HALO, C), F32)
        acts[layer, HALO + N :, :] = jnp.zeros((HALO, C), F32)
    gpad[0:HALO, :] = jnp.zeros((HALO, C), F32)
    gpad[HALO + N :, :] = jnp.zeros((HALO, C), F32)
    for a in range(3):
        for b in range(3):
            w2t[a, b * C : (b + 1) * C, :] = w2_ref[a, b].astype(F32).T.astype(BF16)
    wg[...] = jnp.zeros(wg.shape, F32)
    colpart[...] = jnp.zeros(colpart.shape, F32)

    @pl.loop(1, S)
    def _(step):
        other = lax.rem(s + step, S)
        copy(
            feat_ref, feat_all.at[pl.ds(pl.multiple_of(other * R, R), R)],
            s_feat.at[other], r_feat.at[other], (other, d),
        ).wait_recv()

    CH = min(N, 512)
    for layer in range(LINE_LAYERS):
        e = dil_ref[layer]
        for first in range(0, N, CH):
            if layer == 0:
                h = feat_all[first : first + CH, :].astype(F32)
            else:
                h = h1[first : first + CH, :]
            acts[layer, HALO + first : HALO + first + CH, :] = rounded(gelu_pair(h)[0])
        for first in range(0, N, CH):
            taps = [
                acts[layer, pl.ds(HALO + first + (t - 1) * e, CH), :].astype(BF16)
                for t in range(3)
            ]
            total = dot(taps[0], w1_ref[layer, 0])
            total = total + dot(taps[1], w1_ref[layer, 1])
            total = total + dot(taps[2], w1_ref[layer, 2])
            if layer == 0:
                h1[first : first + CH, :] = rounded(
                    feat_all[first : first + CH, :].astype(F32) + total
                )
            else:
                hid[HOFF + first : HOFF + first + CH, :] = rounded(
                    h1[first : first + CH, :] + total
                )

    for a, b in neighbours:
        @pl.when(exists(a, b))
        def _():
            copy(
                maskt.at[1, 1], maskt.at[1 + a, 1 + b],
                s_mask.at[1 + a, 1 + b], r_mask.at[1 + a, 1 + b], (s + a, d + b),
            ).wait_recv()

    for a in range(3):
        mrow[a, 0:8, :] = maskt[a, 0, 8:16, :]
        mrow[a, 8 : 8 + B // 2, :] = jnp.broadcast_to(maskt[a, 1, 0:1, :], (B // 2, C))
        mrow[a, 8 + B // 2 : 8 + B, :] = jnp.broadcast_to(maskt[a, 1, 8:9, :], (B // 2, C))
        mrow[a, 8 + B : 16 + B, :] = maskt[a, 2, 0:8, :]

    WIDE = B + 2 * HALO

    def band_row(li, kind):
        start = HOFF + row0 - HALO + li
        own = hid[pl.ds(start, 1), :]
        partner = hid[pl.ds(start + d0 - HALO, WIDE), :]
        return rounded(mrow[kind] * 0.5 * (own + partner))

    def spread(target, li, direction):
        for tap in range(3):
            piece = wide[li, pl.ds(HALO + direction * (tap - 1) * e2, B), :]
            target[li, :, tap * C : (tap + 1) * C] = piece.astype(BF16)

    def inner_row(li):
        v = band_row(li, 1)
        value, half = gelu_pair(v)
        wide[li] = rounded(value)
        mid = slice(HALO, HALO + B)
        slope[li - HALO] = slope_from(v[mid], half[mid])
        bandin[li - HALO] = v[mid].astype(BF16)
        spread(p3, li, 1)

    pl.loop(HALO, HALO + R)(inner_row)

    @pl.loop(0, 2 * HALO)
    def _(index):
        low = (index < HALO).astype(jnp.int32)
        li = index + (1 - low) * R
        wide[li] = rounded(gelu_pair(band_row(li, 2 * (1 - low)))[0])
        spread(p3, li, 1)

    def wait_halos(which):
        for a, b in which:
            @pl.when(exists(a, b))
            def _():
                copy(
                    halo_slot(a, b), halo_slot(a, b),
                    s_halo.at[1 + a, 1 + b], r_halo.at[1 + a, 1 + b], (s + a, d + b),
                ).wait_recv()

    wait_halos(sides)

    def gm_row(li, kind, lo, mid, hi):
        wide[li, 0:HALO, :] = mrow[kind, 0:HALO, :] * lo.astype(F32)[8:16]
        wide[li, HALO : HALO + B, :] = mrow[kind, HALO : HALO + B, :] * mid.astype(F32)
        wide[li, HALO + B :, :] = mrow[kind, HALO + B :, :] * hi.astype(F32)[0:8]
        spread(g3, li, -1)

    @pl.loop(0, R)
    def _(i):
        gm_row(i + HALO, 1, left[i], grad_ref[i], right[i])

    KR = 8

    @pl.loop(0, R // KR)
    def _(step):
        i0 = HALO + step * KR
        gm = g3[pl.ds(i0, KR), :, C : 2 * C].reshape(KR * B, C)
        for a in range(3):
            pa = p3[pl.ds(i0 + (a - 1) * e2, KR)].reshape(KR * B, 3 * C)
            wg[a] += dot(gm, pa, ((0,), (0,)))

    for a in range(3):
        for b in range(3):
            wsend[(3 * a + b) * C : (3 * a + b + 1) * C, :] = (
                wg[a, :, b * C : (b + 1) * C].T.astype(BF16)
            )

    def piece_at(owner):
        return pl.ds(pl.multiple_of(owner * PIECE, 16), PIECE)

    def ws_copy(owner, sender):
        return copy(
            wsend.at[piece_at(owner)], wrecv.at[sender],
            s_ws.at[owner], r_ws.at[sender], device(owner),
        )

    @pl.loop(0, NOWN)
    def _(owner):
        @pl.when(owner != me)
        def _():
            ws_copy(owner, me).start()

    @pl.when(me < NOWN)
    def _():
        wrecv[me] = wsend[piece_at(me), :]

    RR = 4

    def back_rows(step):
        i0 = step * RR
        taps = [g3[pl.ds(HALO + i0 - (a - 1) * e2, RR)].reshape(RR * B, 3 * C) for a in range(3)]
        r = dot(taps[0], w2t[0]) + dot(taps[1], w2t[1]) + dot(taps[2], w2t[2])
        r = r.reshape(RR, B, C)
        for k in range(RR):
            gm = g3[HALO + i0 + k, :, C : 2 * C].astype(F32)
            m = mrow[1, HALO : HALO + B, :]
            u = rounded(0.5 * m * (gm + slope[i0 + k] * r[k]))
            rowpart[pl.ds(i0 + k, 1), :] = jnp.sum(u, axis=0, keepdims=True)
            colpart[pl.ds(i0 + k, B), :] += u

    pl.loop(HALO // RR, (R - HALO) // RR)(back_rows)
    wait_halos(edges)

    @pl.loop(0, HALO)
    def _(i):
        gm_row(i, 0, corner[0, 0, i], top[i], corner[0, 1, i])
        gm_row(i + HALO + R, 2, corner[1, 0, i], bottom[i], corner[1, 1, i])

    pl.loop(0, HALO // RR)(back_rows)
    pl.loop((R - HALO) // RR, R // RR)(back_rows)

    PARTS = RATIO + 1

    def g_move(source, slot, target, quarter, index, action):
        dev_is_me = (target == s) & (quarter == d)

        @pl.when((target < S) & jnp.logical_not(dev_is_me))
        def _():
            c = copy(source, gslots.at[slot], s_g.at[index], r_g.at[slot], (target, quarter))
            c.start() if action == "start" else c.wait_send()

        if action == "start":
            @pl.when(dev_is_me)
            def _():
                gslots[slot] = source[...]

    def g_all(action):
        for quarter in range(D):
            g_move(
                rowpart.at[pl.ds(quarter * Q, Q)], d, s, quarter, quarter, action
            )
            for k in range(PARTS):
                g_move(
                    colpart.at[pl.ds(k * R + quarter * Q, Q)],
                    D + d * PARTS + k, s + d * RATIO + k, quarter,
                    D + quarter * PARTS + k, action,
                )

    g_all("start")

    scaling = 1.0 / math.sqrt(N)

    def wa_copy(other, owner):
        return copy(
            wsum, wall.at[piece_at(owner)], s_wa.at[other], r_wa.at[owner], device(other)
        )

    @pl.when(me < NOWN)
    def _():
        @pl.loop(1, NDEV)
        def _(step):
            other = lax.rem(me + step, NDEV)
            ws_copy(me, other).wait_recv()

        total = wrecv[0].astype(F32)
        for k in range(1, NDEV):
            total = total + wrecv[k].astype(F32)
        wsum[...] = (total * scaling).astype(BF16)

        @pl.loop(1, NDEV)
        def _(step):
            wa_copy(lax.rem(me + step, NDEV), me).start()

        wall[piece_at(me), :] = wsum[...]

    @pl.loop(0, R // RR)
    def _(step):
        i0 = step * RR
        taps = [p3[pl.ds(HALO + i0 + (a - 1) * e2, RR)].reshape(RR * B, 3 * C) for a in range(3)]
        q = dot(taps[0], w2_ref[0].reshape(3 * C, C))
        q = q + dot(taps[1], w2_ref[1].reshape(3 * C, C))
        q = q + dot(taps[2], w2_ref[2].reshape(3 * C, C))
        q = q.reshape(RR, B, C)
        for k in range(RR):
            m = mrow[1, HALO : HALO + B, :]
            out_scr[i0 + k] = (m * (bandin[i0 + k].astype(F32) + q[k])).astype(BF16)

    out_copy = pltpu.make_async_copy(out_scr, out_ref, s_out)
    out_copy.start()

    for diag in range(D):
        @pl.when(d != diag)
        def _():
            copy(rowpart.at[pl.ds(0, Q)], gslots.at[diag], s_g.at[0], r_g.at[diag], (s, diag)).wait_recv()

        for k in range(PARTS):
            slot = D + diag * PARTS + k
            source = s - diag * RATIO - k
            remote = (source >= 0) & jnp.logical_not((source == s) & (d == diag))

            @pl.when(remote)
            def _():
                copy(rowpart.at[pl.ds(0, Q)], gslots.at[slot], s_g.at[0], r_g.at[slot], (source, diag)).wait_recv()

            @pl.when(source < 0)
            def _():
                gslots[slot] = jnp.zeros((Q, C), F32)

    gmine[...] = jnp.sum(gslots[...], axis=0).astype(BF16)

    def ga_copy(other, sender):
        return copy(
            gmine, gallb.at[pl.ds(pl.multiple_of(sender * Q, Q), Q)],
            s_ga.at[other], r_ga.at[sender], device(other),
        )

    @pl.loop(1, NDEV)
    def _(step):
        ga_copy(lax.rem(me + step, NDEV), me).start()

    gallb[pl.ds(pl.multiple_of(me * Q, Q), Q), :] = gmine[...]

    @pl.loop(1, NDEV)
    def _(step):
        other = lax.rem(me + step, NDEV)
        ga_copy(other, other).wait_recv()

    gall[...] = gallb[...].astype(F32)

    for layer in reversed(range(LINE_LAYERS)):
        e = dil_ref[layer]
        for first in range(0, N, CH):
            gpad[HALO + first : HALO + first + CH, :] = rounded(gall[first : first + CH, :])
        for t in range(3):
            total = None
            for first in range(0, N, CH):
                tap = acts[layer, pl.ds(HALO + first + (t - 1) * e, CH), :].astype(BF16)
                gb = gpad[HALO + first : HALO + first + CH, :].astype(BF16)
                term = dot(tap, gb, ((0,), (0,)))
                total = term if total is None else total + term
            c1_ref[layer, t] = total * scaling
        for first in range(0, N, CH):
            total = None
            for t in range(3):
                tap = gpad[pl.ds(HALO + first - (t - 1) * e, CH), :].astype(BF16)
                term = dot(tap, w1_ref[layer, t], ((1,), (1,)))
                total = term if total is None else total + term
            if layer == 0:
                h = feat_all[first : first + CH, :].astype(F32)
            else:
                h = h1[first : first + CH, :]
            gall[first : first + CH, :] += slope_from(h, gelu_pair(h)[1]) * total
    seqg_ref[...] = gall[pl.ds(pl.multiple_of(row0, R), R), :]

    @pl.loop(0, NOWN)
    def _(owner):
        @pl.when(owner != me)
        def _():
            wa_copy(me, owner).wait_recv()

    c2_ref[...] = wall[...].astype(F32)

    out_copy.wait()

    @pl.loop(1, S)
    def _(step):
        feat_copy(lax.rem(s + step, S)).wait_send()

    for a, b in neighbours:
        @pl.when(exists(a, b))
        def _():
            mask_copy(a, b).wait_send()
            halo_copy(a, b).wait_send()

    g_all("wait")

    @pl.loop(0, NOWN)
    def _(owner):
        @pl.when(owner != me)
        def _():
            ws_copy(owner, me).wait_send()

    @pl.loop(1, NDEV)
    def _(step):
        other = lax.rem(me + step, NDEV)
        ga_copy(other, me).wait_send()

        @pl.when(me < NOWN)
        def _():
            wa_copy(other, me).wait_send()


def place(parts, *refs):
    count = len(parts)
    sources, targets, sems = refs[:count], refs[count : 2 * count], refs[2 * count]
    copies = []
    for source, target, pieces in zip(sources, targets, parts):
        size = source.shape[0] // pieces
        for k in range(pieces):
            rows = pl.ds(k * size, size)
            copies.append(
                pltpu.make_async_copy(source.at[rows], target.at[rows], sems.at[len(copies)])
            )
    for c in copies:
        c.start()
    for c in copies:
        c.wait()


def body(seq_feat, conv1_weight, conv2_kernel_weight, dilations, block_mask, band_grad):
    S = lax.axis_size("seq")
    D = lax.axis_size("diag")
    R, C = seq_feat.shape
    B = band_grad.shape[1]
    N = R * S
    W = B * D
    NDEV = S * D
    NOWN = owners_for(9 * C // 16, NDEV)
    PIECE = 9 * C // NOWN
    PARTS = B // R + 1
    Q = R // D
    RH, WIDE = R + 2 * HALO, B + 2 * HALO
    vmem = pl.BlockSpec(memory_space=pltpu.VMEM)
    dma = pltpu.SemaphoreType.DMA
    scratch = [
        pltpu.VMEM((N, C), BF16),
        pltpu.VMEM((HOFF + N + W + 32, C), F32),
        pltpu.VMEM((N, C), F32),
        pltpu.VMEM((LINE_LAYERS, N + 2 * HALO, C), F32),
        pltpu.VMEM((3, 3, 16, C), F32),
        pltpu.VMEM((3, WIDE, C), F32),
        pltpu.VMEM((RH, WIDE, C), F32),
        pltpu.VMEM((RH, B, 3 * C), BF16),
        pltpu.VMEM((RH, B, 3 * C), BF16),
        pltpu.VMEM((R, B, C), F32),
        pltpu.VMEM((R, B, C), BF16),
        pltpu.VMEM((3, 3 * C, C), BF16),
        pltpu.VMEM((HALO, B, C), BF16),
        pltpu.VMEM((HALO, B, C), BF16),
        pltpu.VMEM((R, 16, C), BF16),
        pltpu.VMEM((R, 16, C), BF16),
        pltpu.VMEM((2, 2, HALO, 16, C), BF16),
        pltpu.VMEM((3, C, 3 * C), F32),
        pltpu.VMEM((9 * C, C), BF16),
        pltpu.VMEM((NDEV, PIECE, C), BF16),
        pltpu.VMEM((PIECE, C), BF16),
        pltpu.VMEM((9 * C, C), BF16),
        pltpu.VMEM((R, C), F32),
        pltpu.VMEM((R + B, C), F32),
        pltpu.VMEM((D + D * PARTS, Q, C), F32),
        pltpu.VMEM((Q, C), BF16),
        pltpu.VMEM((N, C), F32),
        pltpu.VMEM((N + 2 * HALO, C), F32),
        pltpu.VMEM((N, C), BF16),
        pltpu.VMEM((R, B, C), BF16),
        pltpu.VMEM(conv1_weight.shape, BF16),
        pltpu.VMEM(conv2_kernel_weight.shape, BF16),
        pltpu.SMEM(dilations.shape, jnp.int32),
        pltpu.SMEM(block_mask.shape, jnp.int32),
        pltpu.VMEM((R, B, C), BF16),
        dma((6,)),
        dma((S,)), dma((S,)),
        dma((3, 3)), dma((3, 3)),
        dma((3, 3)), dma((3, 3)),
        dma((NDEV,)), dma((NDEV,)),
        dma((NDEV,)), dma((NDEV,)),
        dma((D + D * PARTS,)), dma((D + D * PARTS,)),
        dma((NDEV,)), dma((NDEV,)), dma,
    ]
    band_out, seq_grad, conv1_grad, conv2_grad = pl.pallas_call(
        functools.partial(kernel, S, D, R, B, C, NOWN),
        out_shape=(
            jax.ShapeDtypeStruct((R, B, C), BF16),
            jax.ShapeDtypeStruct((R, C), F32),
            jax.ShapeDtypeStruct((LINE_LAYERS, 3, C, C), F32),
            jax.ShapeDtypeStruct((9 * C, C), F32),
        ),
        in_specs=[pl.BlockSpec(memory_space=pltpu.HBM)] * 6,
        out_specs=(pl.BlockSpec(memory_space=pl.ANY), vmem, vmem, vmem),
        scratch_shapes=scratch,
        compiler_params=pltpu.CompilerParams(
            collective_id=0, has_side_effects=True, vmem_limit_bytes=min(58 << 20, (48 << 20) + 28 * N * C)
        ),
        name="section",
    )(seq_feat, conv1_weight, conv2_kernel_weight, dilations, block_mask, band_grad)
    results = (band_out, seq_grad, conv1_grad, conv2_grad)
    parts = (8, 1, 2, 3)
    anywhere = pl.BlockSpec(memory_space=pl.ANY)
    band_out, seq_grad, conv1_grad, conv2_grad = pl.pallas_call(
        functools.partial(place, parts),
        out_shape=tuple(jax.ShapeDtypeStruct(x.shape, x.dtype) for x in results),
        in_specs=[anywhere] * 4,
        out_specs=(anywhere,) * 4,
        scratch_shapes=[dma((sum(parts),))],
        compiler_params=pltpu.CompilerParams(vmem_limit_bytes=1024 * 1024),
        name="place",
    )(*results)
    return band_out, seq_grad, conv1_grad, conv2_grad.reshape(3, 3, C, C)


def solution(mesh):
    return jax.shard_map(
        body,
        mesh=mesh,
        in_specs=(P("seq", None), P(), P(), P(), P("seq", "diag"), P("seq", "diag", None)),
        out_specs=(P("seq", "diag", None), P("seq", None), P(), P()),
        check_vma=False,
    )
```

```python
import functools
import math

import jax
import jax.numpy as jnp
from jax import lax
from jax.experimental import pallas as pl
from jax.experimental.pallas import tpu as pltpu
from jax.sharding import PartitionSpec as P

BLOCK = 64
HALO = 8
LINE_LAYERS = 2
HOFF = 16
MESH = pl.DeviceIdType.MESH

root_half = 0.7071067811865476
inv_root_two_pi = 0.3989422804014327

F32 = jnp.float32
BF16 = jnp.bfloat16


def rounded(x):
    return x.astype(BF16).astype(F32)


def gelu_pair(v):
    half = 0.5 * (1.0 + lax.erf(v * root_half))
    return v * half, half


def slope_from(v, half):
    return half + v * jnp.exp(-0.5 * v * v) * inv_root_two_pi


def dot(a, b, dims=((1,), (0,))):
    return lax.dot_general(a, b, (dims, ((), ())), preferred_element_type=F32)


def owners_for(units, devices):
    return max(n for n in range(1, devices + 1) if units % n == 0)


def kernel(
    S, D, R, B, C, NOWN,
    feat_ref, w1_hbm, w2_hbm, dil_hbm, mask_hbm, grad_hbm,
    out_ref, seqg_ref, c1_ref, c2_ref,
    feat_all, hid, h1, acts, maskt, mrow, wide, p3, g3, slope, bandin, w2t,
    top, bottom, left, right, corner,
    wg, wsend, wrecv, wsum, wall, rowpart, colpart, gslots, gmine, gall, gpad, gallb, out_scr,
    w1_ref, w2_ref, dil_ref, mask_ref, grad_ref, s_in,
    s_feat, r_feat, s_halo, r_halo, s_mask, r_mask, s_ws, r_ws, s_wa, r_wa,
    s_g, r_g, s_ga, r_ga, s_out,
):
    N = R * S
    W = B * D
    NDEV = S * D
    PIECE = 9 * C // NOWN
    RATIO = B // R
    Q = R // D
    s = lax.axis_index("seq")
    d = lax.axis_index("diag")
    me = s * D + d
    row0 = s * R
    d0 = d * B

    def device(index):
        return (index // D, index % D)

    def copy(src, dst, ss, rs, dev):
        return pltpu.make_async_remote_copy(
            src_ref=src, dst_ref=dst, send_sem=ss, recv_sem=rs,
            device_id=dev, device_id_type=MESH,
        )

    own_rows = feat_all.at[pl.ds(pl.multiple_of(row0, R), R)]
    loads = [
        pltpu.make_async_copy(source, target, s_in.at[k])
        for k, (source, target) in enumerate(
            [
                (mask_hbm, mask_ref), (dil_hbm, dil_ref), (feat_ref, own_rows),
                (w1_hbm, w1_ref), (w2_hbm, w2_ref), (grad_hbm, grad_ref),
            ]
        )
    ]
    for load in loads:
        load.start()

    loads[0].wait()
    loads[1].wait()
    e2 = dil_ref[LINE_LAYERS]
    for k in range(2):
        value = mask_ref[0, k].astype(F32)
        maskt[1, 1, 8 * k : 8 * k + 8, :] = jnp.full((8, C), 1.0, F32) * value

    barrier = pltpu.get_barrier_semaphore()

    @pl.loop(1, NDEV)
    def _(step):
        pl.semaphore_signal(
            barrier, inc=1, device_id=device(lax.rem(me + step, NDEV)), device_id_type=MESH
        )

    pl.semaphore_wait(barrier, NDEV - 1)

    def feat_copy(other):
        return copy(
            feat_ref, feat_all.at[pl.ds(pl.multiple_of(row0, R), R)],
            s_feat.at[other], r_feat.at[s], (other, d),
        )

    @pl.loop(1, S)
    def _(step):
        feat_copy(lax.rem(s + step, S)).start()

    neighbours = [(a, b) for a in (-1, 0, 1) for b in (-1, 0, 1) if (a, b) != (0, 0)]

    def exists(a, b):
        return (s + a >= 0) & (s + a < S) & (d + b >= 0) & (d + b < D)

    def mask_copy(a, b):
        return copy(
            maskt.at[1, 1], maskt.at[1 - a, 1 - b],
            s_mask.at[1 + a, 1 + b], r_mask.at[1 - a, 1 - b], (s + a, d + b),
        )

    def halo_slot(a, b):
        if b == 0:
            return top if a < 0 else bottom
        if a == 0:
            return left if b < 0 else right
        return corner.at[(1 + a) // 2, (1 + b) // 2]

    def halo_copy(a, b):
        rows = {-1: pl.ds(0, HALO), 0: pl.ds(0, R), 1: pl.ds(R - HALO, HALO)}[a]
        cols = {-1: pl.ds(0, 16), 0: pl.ds(0, B), 1: pl.ds(B - 16, 16)}[b]
        return copy(
            grad_hbm.at[rows, cols], halo_slot(-a, -b),
            s_halo.at[1 + a, 1 + b], r_halo.at[1 - a, 1 - b], (s + a, d + b),
        )

    for a, b in neighbours:
        @pl.when(exists(a, b))
        def _():
            mask_copy(a, b).start()

    sides = [(0, -1), (0, 1)]
    edges = [(-1, 0), (1, 0), (-1, -1), (-1, 1), (1, -1), (1, 1)]
    for a, b in sides + edges:
        @pl.when(exists(a, b))
        def _():
            halo_copy(a, b).start()

        @pl.when(jnp.logical_not(exists(a, b)))
        def _():
            maskt[1 + a, 1 + b] = jnp.zeros((16, C), F32)
            slot = halo_slot(a, b)
            slot[...] = jnp.zeros(slot.shape, BF16)

    for load in loads[2:]:
        load.wait()
    hid[0:HOFF, :] = jnp.zeros((HOFF, C), F32)
    hid[HOFF + N :, :] = jnp.zeros((hid.shape[0] - HOFF - N, C), F32)
    for layer in range(LINE_LAYERS):
        acts[layer, 0:HALO, :] = jnp.zeros((HALO, C), F32)
        acts[layer, HALO + N :, :] = jnp.zeros((HALO, C), F32)
    gpad[0:HALO, :] = jnp.zeros((HALO, C), F32)
    gpad[HALO + N :, :] = jnp.zeros((HALO, C), F32)
    for a in range(3):
        for b in range(3):
            w2t[a, b * C : (b + 1) * C, :] = w2_ref[a, b].astype(F32).T.astype(BF16)
    wg[...] = jnp.zeros(wg.shape, F32)
    colpart[...] = jnp.zeros(colpart.shape, F32)

    @pl.loop(1, S)
    def _(step):
        other = lax.rem(s + step, S)
        copy(
            feat_ref, feat_all.at[pl.ds(pl.multiple_of(other * R, R), R)],
            s_feat.at[other], r_feat.at[other], (other, d),
        ).wait_recv()

    CH = min(N, 512)
    for layer in range(LINE_LAYERS):
        e = dil_ref[layer]
        for first in range(0, N, CH):
            if layer == 0:
                h = feat_all[first : first + CH, :].astype(F32)
            else:
                h = h1[first : first + CH, :]
            acts[layer, HALO + first : HALO + first + CH, :] = rounded(gelu_pair(h)[0])
        for first in range(0, N, CH):
            taps = [
                acts[layer, pl.ds(HALO + first + (t - 1) * e, CH), :].astype(BF16)
                for t in range(3)
            ]
            total = dot(taps[0], w1_ref[layer, 0])
            total = total + dot(taps[1], w1_ref[layer, 1])
            total = total + dot(taps[2], w1_ref[layer, 2])
            if layer == 0:
                h1[first : first + CH, :] = rounded(
                    feat_all[first : first + CH, :].astype(F32) + total
                )
            else:
                hid[HOFF + first : HOFF + first + CH, :] = rounded(
                    h1[first : first + CH, :] + total
                )

    for a, b in neighbours:
        @pl.when(exists(a, b))
        def _():
            copy(
                maskt.at[1, 1], maskt.at[1 + a, 1 + b],
                s_mask.at[1 + a, 1 + b], r_mask.at[1 + a, 1 + b], (s + a, d + b),
            ).wait_recv()

    for a in range(3):
        mrow[a, 0:8, :] = maskt[a, 0, 8:16, :]
        mrow[a, 8 : 8 + B // 2, :] = jnp.broadcast_to(maskt[a, 1, 0:1, :], (B // 2, C))
        mrow[a, 8 + B // 2 : 8 + B, :] = jnp.broadcast_to(maskt[a, 1, 8:9, :], (B // 2, C))
        mrow[a, 8 + B : 16 + B, :] = maskt[a, 2, 0:8, :]

    WIDE = B + 2 * HALO

    def band_row(li, kind):
        start = HOFF + row0 - HALO + li
        own = hid[pl.ds(start, 1), :]
        partner = hid[pl.ds(start + d0 - HALO, WIDE), :]
        return rounded(mrow[kind] * 0.5 * (own + partner))

    def spread(target, li, direction):
        for tap in range(3):
            piece = wide[li, pl.ds(HALO + direction * (tap - 1) * e2, B), :]
            target[li, :, tap * C : (tap + 1) * C] = piece.astype(BF16)

    def inner_row(li):
        v = band_row(li, 1)
        value, half = gelu_pair(v)
        wide[li] = rounded(value)
        mid = slice(HALO, HALO + B)
        slope[li - HALO] = slope_from(v[mid], half[mid])
        bandin[li - HALO] = v[mid].astype(BF16)
        spread(p3, li, 1)

    pl.loop(HALO, HALO + R)(inner_row)

    @pl.loop(0, 2 * HALO)
    def _(index):
        low = (index < HALO).astype(jnp.int32)
        li = index + (1 - low) * R
        wide[li] = rounded(gelu_pair(band_row(li, 2 * (1 - low)))[0])
        spread(p3, li, 1)

    def wait_halos(which):
        for a, b in which:
            @pl.when(exists(a, b))
            def _():
                copy(
                    halo_slot(a, b), halo_slot(a, b),
                    s_halo.at[1 + a, 1 + b], r_halo.at[1 + a, 1 + b], (s + a, d + b),
                ).wait_recv()

    wait_halos(sides)

    def gm_row(li, kind, lo, mid, hi):
        wide[li, 0:HALO, :] = mrow[kind, 0:HALO, :] * lo.astype(F32)[8:16]
        wide[li, HALO : HALO + B, :] = mrow[kind, HALO : HALO + B, :] * mid.astype(F32)
        wide[li, HALO + B :, :] = mrow[kind, HALO + B :, :] * hi.astype(F32)[0:8]
        spread(g3, li, -1)

    @pl.loop(0, R)
    def _(i):
        gm_row(i + HALO, 1, left[i], grad_ref[i], right[i])

    KR = 8

    @pl.loop(0, R // KR)
    def _(step):
        i0 = HALO + step * KR
        gm = g3[pl.ds(i0, KR), :, C : 2 * C].reshape(KR * B, C)
        for a in range(3):
            pa = p3[pl.ds(i0 + (a - 1) * e2, KR)].reshape(KR * B, 3 * C)
            wg[a] += dot(gm, pa, ((0,), (0,)))

    for a in range(3):
        for b in range(3):
            wsend[(3 * a + b) * C : (3 * a + b + 1) * C, :] = (
                wg[a, :, b * C : (b + 1) * C].T.astype(BF16)
            )

    def piece_at(owner):
        return pl.ds(pl.multiple_of(owner * PIECE, 16), PIECE)

    def ws_copy(owner, sender):
        return copy(
            wsend.at[piece_at(owner)], wrecv.at[sender],
            s_ws.at[owner], r_ws.at[sender], device(owner),
        )

    @pl.loop(0, NOWN)
    def _(owner):
        @pl.when(owner != me)
        def _():
            ws_copy(owner, me).start()

    @pl.when(me < NOWN)
    def _():
        wrecv[me] = wsend[piece_at(me), :]

    RR = 8

    def back_rows(step):
        i0 = step * RR
        taps = [g3[pl.ds(HALO + i0 - (a - 1) * e2, RR)].reshape(RR * B, 3 * C) for a in range(3)]
        r = dot(taps[0], w2t[0]) + dot(taps[1], w2t[1]) + dot(taps[2], w2t[2])
        r = r.reshape(RR, B, C)
        for k in range(RR):
            gm = g3[HALO + i0 + k, :, C : 2 * C].astype(F32)
            m = mrow[1, HALO : HALO + B, :]
            u = rounded(0.5 * m * (gm + slope[i0 + k] * r[k]))
            rowpart[pl.ds(i0 + k, 1), :] = jnp.sum(u, axis=0, keepdims=True)
            colpart[pl.ds(i0 + k, B), :] += u

    pl.loop(HALO // RR, (R - HALO) // RR)(back_rows)
    wait_halos(edges)

    @pl.loop(0, HALO)
    def _(i):
        gm_row(i, 0, corner[0, 0, i], top[i], corner[0, 1, i])
        gm_row(i + HALO + R, 2, corner[1, 0, i], bottom[i], corner[1, 1, i])

    pl.loop(0, HALO // RR)(back_rows)
    pl.loop((R - HALO) // RR, R // RR)(back_rows)

    PARTS = RATIO + 1

    def g_move(source, slot, target, quarter, index, action):
        dev_is_me = (target == s) & (quarter == d)

        @pl.when((target < S) & jnp.logical_not(dev_is_me))
        def _():
            c = copy(source, gslots.at[slot], s_g.at[index], r_g.at[slot], (target, quarter))
            c.start() if action == "start" else c.wait_send()

        if action == "start":
            @pl.when(dev_is_me)
            def _():
                gslots[slot] = source[...]

    def g_all(action):
        for quarter in range(D):
            g_move(
                rowpart.at[pl.ds(quarter * Q, Q)], d, s, quarter, quarter, action
            )
            for k in range(PARTS):
                g_move(
                    colpart.at[pl.ds(k * R + quarter * Q, Q)],
                    D + d * PARTS + k, s + d * RATIO + k, quarter,
                    D + quarter * PARTS + k, action,
                )

    g_all("start")

    scaling = 1.0 / math.sqrt(N)

    def wa_copy(other, owner):
        return copy(
            wsum, wall.at[piece_at(owner)], s_wa.at[other], r_wa.at[owner], device(other)
        )

    @pl.when(me < NOWN)
    def _():
        @pl.loop(1, NDEV)
        def _(step):
            other = lax.rem(me + step, NDEV)
            ws_copy(me, other).wait_recv()

        total = wrecv[0].astype(F32)
        for k in range(1, NDEV):
            total = total + wrecv[k].astype(F32)
        wsum[...] = (total * scaling).astype(BF16)

        @pl.loop(1, NDEV)
        def _(step):
            wa_copy(lax.rem(me + step, NDEV), me).start()

        wall[piece_at(me), :] = wsum[...]

    @pl.loop(0, R // RR)
    def _(step):
        i0 = step * RR
        taps = [p3[pl.ds(HALO + i0 + (a - 1) * e2, RR)].reshape(RR * B, 3 * C) for a in range(3)]
        q = dot(taps[0], w2_ref[0].reshape(3 * C, C))
        q = q + dot(taps[1], w2_ref[1].reshape(3 * C, C))
        q = q + dot(taps[2], w2_ref[2].reshape(3 * C, C))
        q = q.reshape(RR, B, C)
        for k in range(RR):
            m = mrow[1, HALO : HALO + B, :]
            out_scr[i0 + k] = (m * (bandin[i0 + k].astype(F32) + q[k])).astype(BF16)

    out_copy = pltpu.make_async_copy(out_scr, out_ref, s_out)
    out_copy.start()

    for diag in range(D):
        @pl.when(d != diag)
        def _():
            copy(rowpart.at[pl.ds(0, Q)], gslots.at[diag], s_g.at[0], r_g.at[diag], (s, diag)).wait_recv()

        for k in range(PARTS):
            slot = D + diag * PARTS + k
            source = s - diag * RATIO - k
            remote = (source >= 0) & jnp.logical_not((source == s) & (d == diag))

            @pl.when(remote)
            def _():
                copy(rowpart.at[pl.ds(0, Q)], gslots.at[slot], s_g.at[0], r_g.at[slot], (source, diag)).wait_recv()

            @pl.when(source < 0)
            def _():
                gslots[slot] = jnp.zeros((Q, C), F32)

    gmine[...] = jnp.sum(gslots[...], axis=0).astype(BF16)

    def ga_copy(other, sender):
        return copy(
            gmine, gallb.at[pl.ds(pl.multiple_of(sender * Q, Q), Q)],
            s_ga.at[other], r_ga.at[sender], device(other),
        )

    @pl.loop(1, NDEV)
    def _(step):
        ga_copy(lax.rem(me + step, NDEV), me).start()

    gallb[pl.ds(pl.multiple_of(me * Q, Q), Q), :] = gmine[...]

    @pl.loop(1, NDEV)
    def _(step):
        other = lax.rem(me + step, NDEV)
        ga_copy(other, other).wait_recv()

    gall[...] = gallb[...].astype(F32)

    for layer in reversed(range(LINE_LAYERS)):
        e = dil_ref[layer]
        for first in range(0, N, CH):
            gpad[HALO + first : HALO + first + CH, :] = rounded(gall[first : first + CH, :])
        for t in range(3):
            total = None
            for first in range(0, N, CH):
                tap = acts[layer, pl.ds(HALO + first + (t - 1) * e, CH), :].astype(BF16)
                gb = gpad[HALO + first : HALO + first + CH, :].astype(BF16)
                term = dot(tap, gb, ((0,), (0,)))
                total = term if total is None else total + term
            c1_ref[layer, t] = total * scaling
        for first in range(0, N, CH):
            total = None
            for t in range(3):
                tap = gpad[pl.ds(HALO + first - (t - 1) * e, CH), :].astype(BF16)
                term = dot(tap, w1_ref[layer, t], ((1,), (1,)))
                total = term if total is None else total + term
            if layer == 0:
                h = feat_all[first : first + CH, :].astype(F32)
            else:
                h = h1[first : first + CH, :]
            gall[first : first + CH, :] += slope_from(h, gelu_pair(h)[1]) * total
    seqg_ref[...] = gall[pl.ds(pl.multiple_of(row0, R), R), :]

    @pl.loop(0, NOWN)
    def _(owner):
        @pl.when(owner != me)
        def _():
            wa_copy(me, owner).wait_recv()

    c2_ref[...] = wall[...].astype(F32)

    out_copy.wait()

    @pl.loop(1, S)
    def _(step):
        feat_copy(lax.rem(s + step, S)).wait_send()

    for a, b in neighbours:
        @pl.when(exists(a, b))
        def _():
            mask_copy(a, b).wait_send()
            halo_copy(a, b).wait_send()

    g_all("wait")

    @pl.loop(0, NOWN)
    def _(owner):
        @pl.when(owner != me)
        def _():
            ws_copy(owner, me).wait_send()

    @pl.loop(1, NDEV)
    def _(step):
        other = lax.rem(me + step, NDEV)
        ga_copy(other, me).wait_send()

        @pl.when(me < NOWN)
        def _():
            wa_copy(other, me).wait_send()


def place(parts, *refs):
    count = len(parts)
    sources, targets, sems = refs[:count], refs[count : 2 * count], refs[2 * count]
    copies = []
    for source, target, pieces in zip(sources, targets, parts):
        size = source.shape[0] // pieces
        for k in range(pieces):
            rows = pl.ds(k * size, size)
            copies.append(
                pltpu.make_async_copy(source.at[rows], target.at[rows], sems.at[len(copies)])
            )
    for c in copies:
        c.start()
    for c in copies:
        c.wait()


def body(seq_feat, conv1_weight, conv2_kernel_weight, dilations, block_mask, band_grad):
    S = lax.axis_size("seq")
    D = lax.axis_size("diag")
    R, C = seq_feat.shape
    B = band_grad.shape[1]
    N = R * S
    W = B * D
    NDEV = S * D
    NOWN = owners_for(9 * C // 16, NDEV)
    PIECE = 9 * C // NOWN
    PARTS = B // R + 1
    Q = R // D
    RH, WIDE = R + 2 * HALO, B + 2 * HALO
    vmem = pl.BlockSpec(memory_space=pltpu.VMEM)
    dma = pltpu.SemaphoreType.DMA
    scratch = [
        pltpu.VMEM((N, C), BF16),
        pltpu.VMEM((HOFF + N + W + 32, C), F32),
        pltpu.VMEM((N, C), F32),
        pltpu.VMEM((LINE_LAYERS, N + 2 * HALO, C), F32),
        pltpu.VMEM((3, 3, 16, C), F32),
        pltpu.VMEM((3, WIDE, C), F32),
        pltpu.VMEM((RH, WIDE, C), F32),
        pltpu.VMEM((RH, B, 3 * C), BF16),
        pltpu.VMEM((RH, B, 3 * C), BF16),
        pltpu.VMEM((R, B, C), F32),
        pltpu.VMEM((R, B, C), BF16),
        pltpu.VMEM((3, 3 * C, C), BF16),
        pltpu.VMEM((HALO, B, C), BF16),
        pltpu.VMEM((HALO, B, C), BF16),
        pltpu.VMEM((R, 16, C), BF16),
        pltpu.VMEM((R, 16, C), BF16),
        pltpu.VMEM((2, 2, HALO, 16, C), BF16),
        pltpu.VMEM((3, C, 3 * C), F32),
        pltpu.VMEM((9 * C, C), BF16),
        pltpu.VMEM((NDEV, PIECE, C), BF16),
        pltpu.VMEM((PIECE, C), BF16),
        pltpu.VMEM((9 * C, C), BF16),
        pltpu.VMEM((R, C), F32),
        pltpu.VMEM((R + B, C), F32),
        pltpu.VMEM((D + D * PARTS, Q, C), F32),
        pltpu.VMEM((Q, C), BF16),
        pltpu.VMEM((N, C), F32),
        pltpu.VMEM((N + 2 * HALO, C), F32),
        pltpu.VMEM((N, C), BF16),
        pltpu.VMEM((R, B, C), BF16),
        pltpu.VMEM(conv1_weight.shape, BF16),
        pltpu.VMEM(conv2_kernel_weight.shape, BF16),
        pltpu.SMEM(dilations.shape, jnp.int32),
        pltpu.SMEM(block_mask.shape, jnp.int32),
        pltpu.VMEM((R, B, C), BF16),
        dma((6,)),
        dma((S,)), dma((S,)),
        dma((3, 3)), dma((3, 3)),
        dma((3, 3)), dma((3, 3)),
        dma((NDEV,)), dma((NDEV,)),
        dma((NDEV,)), dma((NDEV,)),
        dma((D + D * PARTS,)), dma((D + D * PARTS,)),
        dma((NDEV,)), dma((NDEV,)), dma,
    ]
    band_out, seq_grad, conv1_grad, conv2_grad = pl.pallas_call(
        functools.partial(kernel, S, D, R, B, C, NOWN),
        out_shape=(
            jax.ShapeDtypeStruct((R, B, C), BF16),
            jax.ShapeDtypeStruct((R, C), F32),
            jax.ShapeDtypeStruct((LINE_LAYERS, 3, C, C), F32),
            jax.ShapeDtypeStruct((9 * C, C), F32),
        ),
        in_specs=[pl.BlockSpec(memory_space=pltpu.HBM)] * 6,
        out_specs=(pl.BlockSpec(memory_space=pl.ANY), vmem, vmem, vmem),
        scratch_shapes=scratch,
        compiler_params=pltpu.CompilerParams(
            collective_id=0, has_side_effects=True, vmem_limit_bytes=min(58 << 20, (48 << 20) + 28 * N * C)
        ),
        name="section",
    )(seq_feat, conv1_weight, conv2_kernel_weight, dilations, block_mask, band_grad)
    results = (band_out, seq_grad, conv1_grad, conv2_grad)
    parts = (8, 1, 2, 3)
    anywhere = pl.BlockSpec(memory_space=pl.ANY)
    band_out, seq_grad, conv1_grad, conv2_grad = pl.pallas_call(
        functools.partial(place, parts),
        out_shape=tuple(jax.ShapeDtypeStruct(x.shape, x.dtype) for x in results),
        in_specs=[anywhere] * 4,
        out_specs=(anywhere,) * 4,
        scratch_shapes=[dma((sum(parts),))],
        compiler_params=pltpu.CompilerParams(vmem_limit_bytes=1024 * 1024),
        name="place",
    )(*results)
    return band_out, seq_grad, conv1_grad, conv2_grad.reshape(3, 3, C, C)


def solution(mesh):
    return jax.shard_map(
        body,
        mesh=mesh,
        in_specs=(P("seq", None), P(), P(), P(), P("seq", "diag"), P("seq", "diag", None)),
        out_specs=(P("seq", "diag", None), P("seq", None), P(), P()),
        check_vma=False,
    )
```
